512 devices in a mesh: row: 16 (over y, core), col: 32 (over x, z).
Axes of the slice: x: 4, y: 8, z: 8, core: 2. Of those that a mesh axis runs over, the one named last changes fastest.
Arguments:
- pointing_dirty_images: bfloat16 [512, 1024, 1024], P(('row', 'col')), may hold values from -6 to 6
- beam_coefs: bfloat16 [512, 36], P(('row', 'col'))
- pointing_offsets: int32 [512, 2], P(('row', 'col')), may hold values from 0 to 60, as said below
Outputs:
- joint_image: bfloat16 [64, 32, 256, 256], P('row', 'col')
- residual: bfloat16 [512, 1024, 1024], P(('row', 'col'))
The draws below stay inside these ranges and needn't reach their ends.
Inputs may be any that keep to these rules, and one draw needn't show every extreme that they name: `pointing_offsets`: for a pointing p in group g = p // 32: the tile row lies in 4 g .. 4 g + 3, and equals 4 g in the last group; the tile column lies in 0 .. 28; the first pointing of each group has column 0 and the second column 28.
All inputs are finite; a program needn't handle non-finite values.
Results may differ from the reference program's by a relative error of at most 0.005.
Values may be sent and summed in bfloat16 or wider, within the bound.
A program may use at most 128 MiB of HBM per device.

```python
import math
import jax
import jax.numpy as jnp
import numpy as np
from jax import lax

TILE = 256
FT = 4
ZT = 36
FOOT = 1024
POINTINGS = 512
MROWS = 64
N_ROW = 16
N_COL = 32


def term_degrees():
    listing = []
    for degree in range(8):
        for azimuth in range(-degree, degree + 1, 2):
            listing.append(degree)
    return np.array(listing, dtype=np.float32)


def draw_beam_coefs(key, part):
    key = jax.random.fold_in(key, 1)
    degrees = jnp.asarray(term_degrees())
    first_key, second_key = jax.random.split(key)
    noise = jax.random.normal(first_key, (POINTINGS, ZT), jnp.float32)
    scales = 0.25 / (1.0 + degrees)
    piston = 1.0 + 0.1 * jax.random.uniform(second_key, (POINTINGS, 1), jnp.float32, -1.0, 1.0)
    values = noise * scales[None, :]
    values = jnp.concatenate([piston, values[:, 1:]], axis=1)
    return values.astype(jnp.bfloat16)


def draw_pointing_offsets(key, part):
    key = jax.random.fold_in(key, 2)
    keys = jax.random.split(key, 5)
    counter = jnp.arange(POINTINGS, dtype=jnp.int32)
    group = counter // N_COL
    within = counter % N_COL
    jitter = jax.random.randint(keys[0], (POINTINGS,), 0, FT)
    top_row = FT * group + jnp.where(group < N_ROW - 1, jitter, 0)
    centre = jax.random.randint(keys[1], (N_ROW,), 0, N_COL - FT + 1)[group]
    spread = jax.random.randint(keys[2], (POINTINGS,), -2, 3)
    anywhere = jax.random.randint(keys[3], (POINTINGS,), 0, N_COL - FT + 1)
    pick = jax.random.randint(keys[4], (POINTINGS,), 0, 2)
    left_neighbour = jnp.where(pick == 0, anywhere, jnp.clip(centre + spread, 0, N_COL - FT))
    left_neighbour = jnp.where(within == 0, 0, jnp.where(within == 1, N_COL - FT, left_neighbour))
    return jnp.stack([top_row, left_neighbour], axis=1).astype(jnp.int32)


def steps_of(own_key, shape, shards, least, high):
    def one(axis_at, parts):
        draws = jax.random.uniform(jax.random.fold_in(jax.random.fold_in(own_key, 6), axis_at), (parts,), jnp.float32, least / len(shards), high / len(shards))
        return jnp.repeat(jnp.exp(draws), shape[axis_at] // parts).reshape((-1,) + (1,) * (len(shape) - axis_at - 1))

    gain = one(*shards[0])
    for cut in shards[1:]:
        gain = gain * one(*cut)
    return gain


def gaussian(key, shape, scale, limit, pieces=(), kind=jnp.bfloat16):
    drawn = scale * jax.random.normal(key, shape, jnp.float32)
    if pieces:
        drawn = drawn * steps_of(key, shape, pieces, -0.22, 0.18)
    return jnp.clip(drawn, -limit, limit).astype(kind)


def setup_inputs(seed: int = 0) -> dict:
    splits = jax.random.split(jax.random.key(seed), 4)
    return {
        "pointing_dirty_images": gaussian(splits[0], (POINTINGS, FOOT, FOOT), 1.0, 6.0, ((0, 512),)),
        "beam_coefs": draw_beam_coefs(jax.random.fold_in(splits[3], 71), 0),
        "pointing_offsets": draw_pointing_offsets(jax.random.fold_in(splits[3], 71), 0),
    }


weight_floor = 0.1

def zernike_table():
    table = np.zeros((36, 8, 8))
    term = 0
    for degree in range(8):
        for azimuth in range(-degree, degree + 1, 2):
            order = abs(azimuth)
            angular = np.zeros((8, 8))
            for power in range(order + 1):
                weight = math.comb(order, power)
                if azimuth >= 0 and power % 2 == 0:
                    angular[order - power, power] += weight * (-1) ** (power // 2)
                if azimuth < 0 and power % 2 == 1:
                    angular[order - power, power] += weight * (-1) ** ((power - 1) // 2)
            for stepper in range((degree - order) // 2 + 1):
                radial = (-1) ** stepper * math.factorial(degree - stepper) / (math.factorial(stepper) * math.factorial((degree + order) // 2 - stepper) * math.factorial((degree - order) // 2 - stepper))
                square_power = (degree - 2 * stepper - order) // 2
                for portion in range(square_power + 1):
                    factor = radial * math.comb(square_power, portion)
                    shift_u = 2 * portion
                    shift_v = 2 * (square_power - portion)
                    table[term, shift_u:, shift_v:] += factor * angular[:8 - shift_u, :8 - shift_v]
            term += 1
    return table

def positions(start, count, footprint):
    pixels = start + jnp.arange(count, dtype=jnp.float32)
    return (pixels + 0.5 - footprint / 2.0) * (math.sqrt(2.0) / footprint)

def beam_power(coef, table, across, shift_downward_step):
    monomial_term = jnp.einsum('k,kab->ab', coef.astype(jnp.float32), table, precision=lax.Precision.HIGHEST)
    exponent_value = jnp.arange(8, dtype=jnp.float32)
    upow = across[None, :] ** exponent_value[:, None]
    vertical_power = shift_downward_step[None, :] ** exponent_value[:, None]
    left_neighbour = jnp.dot(vertical_power.T, monomial_term.T, precision=lax.Precision.HIGHEST)
    field = jnp.dot(left_neighbour, upow, precision=lax.Precision.HIGHEST)
    return (field * field).astype(jnp.bfloat16)

def split_tiles(picture):
    side = picture.shape[0] // FT
    return picture.reshape(FT, side, FT, side).transpose(0, 2, 1, 3).reshape(FT * FT, side, side)

def join_tiles(tiles):
    side = tiles.shape[1]
    return tiles.reshape(FT, FT, side, side).transpose(0, 2, 1, 3).reshape(FT * side, FT * side)

def tile_targets(offset):
    counter = jnp.arange(FT * FT, dtype=jnp.int32)
    rows_abs = offset[0] + counter // FT
    cols_abs = offset[1] + counter % FT
    slots = (cols_abs + FT * rows_abs) % N_COL
    return (rows_abs.astype(jnp.int32), slots.astype(jnp.int32))

def reference(pointing_dirty_images, beam_coefs, pointing_offsets):
    table = jnp.asarray(zernike_table(), jnp.float32)
    across = positions(0.0, FOOT, FOOT)

    def power_of(coef):
        return beam_power(coef, table, across, across)

    def accumulate(carry, inputs):
        numer, weigh = carry
        picture, coef, offset = inputs
        power = split_tiles(power_of(coef)).astype(jnp.float32)
        values = split_tiles(picture).astype(jnp.float32)
        rows_abs, slots = tile_targets(offset)
        numer = numer.at[rows_abs, slots].add(values * power)
        weigh = weigh.at[rows_abs, slots].add(power * power)
        return ((numer, weigh), None)
    zeros = jnp.zeros((MROWS, N_COL, TILE, TILE), jnp.float32)
    (numer, weigh), unused = lax.scan(accumulate, (zeros, zeros), (pointing_dirty_images, beam_coefs, pointing_offsets))
    joint_image = (numer / jnp.maximum(weigh, weight_floor)).astype(jnp.bfloat16)

    def residual_of(inputs):
        picture, coef, offset = inputs
        power = split_tiles(power_of(coef)).astype(jnp.float32)
        values = split_tiles(picture).astype(jnp.float32)
        rows_abs, slots = tile_targets(offset)
        model = joint_image[rows_abs, slots].astype(jnp.float32)
        return join_tiles((values - power * model).astype(jnp.bfloat16))
    residual = lax.map(residual_of, (pointing_dirty_images, beam_coefs, pointing_offsets))
    return (joint_image, residual)
```

```python
import functools
import math

import jax
import jax.numpy as jnp
import numpy as np
from jax import lax
from jax.experimental import pallas as pl
from jax.experimental.pallas import tpu as pltpu
from jax.sharding import PartitionSpec as P

MESH = pl.DeviceIdType.MESH
FT = 4
NPEER = 32
RES = 16
ROWS7 = 7
NT = 2 * ROWS7
GR = 16
SHARED = 3 * 2 * GR
FLOOR = 0.1
HIGHEST = lax.Precision.HIGHEST
F32 = jnp.float32
BF16 = jnp.bfloat16


def zernike_table():
    table = np.zeros((36, 8, 8))
    term = 0
    for degree in range(8):
        for azimuth in range(-degree, degree + 1, 2):
            order = abs(azimuth)
            angular = np.zeros((8, 8))
            for power in range(order + 1):
                weight = math.comb(order, power)
                if azimuth >= 0 and power % 2 == 0:
                    angular[order - power, power] += weight * (-1) ** (power // 2)
                if azimuth < 0 and power % 2 == 1:
                    angular[order - power, power] += weight * (-1) ** ((power - 1) // 2)
            for step in range((degree - order) // 2 + 1):
                radial = (
                    (-1) ** step
                    * math.factorial(degree - step)
                    / (
                        math.factorial(step)
                        * math.factorial((degree + order) // 2 - step)
                        * math.factorial((degree - order) // 2 - step)
                    )
                )
                square = (degree - 2 * step - order) // 2
                for part in range(square + 1):
                    su, sv = 2 * part, 2 * (square - part)
                    table[term, su:, sv:] += (
                        radial * math.comb(square, part) * angular[: 8 - su, : 8 - sv]
                    )
            term += 1
    return table


def to_local_table(tile):
    foot = FT * tile
    table = zernike_table()
    unit = math.sqrt(2.0) / foot
    sigma = unit * tile / 2
    shift = np.zeros((FT, 8, 8))
    for a in range(FT):
        centre = (a * tile + tile / 2 - foot / 2) * unit
        for i in range(8):
            for m in range(i + 1):
                shift[a, i, m] = math.comb(i, m) * centre ** (i - m) * sigma**m
    local = np.einsum("kij,bim,ajn->kabnm", table, shift, shift)
    to_local = np.zeros((36, RES, 128))
    to_local[:, :, :64] = local.reshape(36, RES, 64)
    return to_local.reshape(36, RES * 128).astype(np.float32)


def iota(shape, dim):
    return lax.broadcasted_iota(jnp.int32, shape, dim)


def to_power(base, exponent):
    square = base * base
    low = jnp.where(lax.rem(exponent, 2) == 1, base, 1.0)
    middle = jnp.where(lax.rem(lax.div(exponent, 2), 2) == 1, square, 1.0)
    return low * middle * jnp.where(lax.div(exponent, 4) == 1, square * square, 1.0)


def kernel(
    strips,
    send,
    meta_send,
    joint_hbm,
    ret_recv,
    recv,
    pbuf,
    ret_send,
    meta_recv,
    bbuf,
    xbuf,
    wbuf,
    k2,
    kt,
    rhs,
    weigh,
    w_lo,
    w_hi,
    numer,
    n_lo,
    n_hi,
    ibuf,
    jbuf,
    fwd_s,
    fwd_r,
    fwd_l,
    meta_s,
    meta_r,
    meta_l,
    w_s,
    w_r,
    n_s,
    n_r,
    j_s,
    j_r,
    j_l,
    ret_s,
    ret_r,
    ret_l,
):
    row = lax.axis_index("row")
    col = lax.axis_index("col")
    n_row = lax.axis_size("row")
    tile = recv.shape[-1]
    half = tile // 2
    rr = half // strips
    gg = rr // GR
    groups = half // GR
    nx, nz = NPEER // 8, 8
    px, pz = lax.div(col, nz), lax.rem(col, nz)
    side = lax.div(col, RES)
    up = lax.rem(row + 1, n_row)
    below = lax.rem(row + n_row - 1, n_row)
    partner = lax.rem(col + RES, NPEER)

    def peer(i):
        j = lax.div(i, nx)
        last = lax.div(j, nz - 1)
        near = lax.div(j, 2) + 1
        dz = (near + lax.rem(j, 2) * (nz - 2 * near)) * (1 - last)
        e = lax.rem(i + last, nx)
        dx = e + lax.div(e, 2) * (1 - 2 * lax.rem(e, 2))
        return lax.rem(px + dx, nx) * nz + lax.rem(pz + dz, nz)

    barrier = pltpu.get_barrier_semaphore()

    def greet(i, carry):
        pl.semaphore_signal(barrier, inc=1, device_id=(row, peer(i)), device_id_type=MESH)
        return carry

    lax.fori_loop(0, NPEER - 1, greet, 0)
    pl.semaphore_signal(barrier, inc=1, device_id=(up, col), device_id_type=MESH)
    pl.semaphore_signal(barrier, inc=1, device_id=(below, col), device_id_type=MESH)

    def own_tile(s):
        return pltpu.make_async_copy(send.at[col, s], recv.at[s, col], fwd_l.at[s])

    def own_meta():
        return pltpu.make_async_copy(meta_send.at[lax.rem(col, RES)], meta_recv.at[col], meta_l)

    def own_residual(s):
        return pltpu.make_async_copy(ret_send.at[s, col], ret_recv.at[col, s], ret_l.at[s])

    def forward(s):
        def one(i, carry):
            to = peer(i)
            pltpu.make_async_remote_copy(
                src_ref=send.at[to, s],
                dst_ref=recv.at[s, col],
                send_sem=fwd_s.at[s],
                recv_sem=fwd_r.at[s],
                device_id=(row, to),
                device_id_type=MESH,
            ).start()
            return carry

        lax.fori_loop(0, NPEER - 1, one, 0)
        own_tile(s).start()

    def send_meta(i, carry):
        to = peer(i)
        pltpu.make_async_remote_copy(
            src_ref=meta_send.at[lax.rem(to, RES)],
            dst_ref=meta_recv.at[col],
            send_sem=meta_s,
            recv_sem=meta_r,
            device_id=(row, to),
            device_id_type=MESH,
        ).start()
        return carry

    pl.semaphore_wait(barrier, NPEER + 1)
    lax.fori_loop(0, NPEER - 1, send_meta, 0)
    own_meta().start()

    def forward_strip(s, carry):
        forward(s)
        return carry

    lax.fori_loop(0, strips, forward_strip, 0)

    shape = (128, tile)
    spot = (iota(shape, 1).astype(F32) + (0.5 - tile / 2)) * (2.0 / tile)
    across = jnp.where(iota(shape, 0) < 64, to_power(spot, lax.rem(iota(shape, 0), 8)), 0.0)
    shape = (half, 48)
    spot = ((iota(shape, 0) + side * half).astype(F32) + (0.5 - tile / 2)) * (2.0 / tile)
    whole = to_power(spot, lax.rem(iota(shape, 1), 8))
    first = whole.astype(BF16).astype(F32)
    second = (whole - first).astype(BF16).astype(F32)
    third = whole - first - second
    part = lax.div(iota(shape, 1), 8)
    down = jnp.where(
        part == 5, third, jnp.where(jnp.logical_or(part == 2, part == 4), second, first)
    ).astype(BF16)
    shape = (256, 128)
    spread = jnp.where(iota(shape, 1) == 64 + lax.div(iota(shape, 0), GR), 1.0, 0.0).astype(BF16)

    arrived = meta_recv.at[pl.ds(0, NPEER - 1)]
    pltpu.make_async_copy(arrived, arrived, meta_r).wait()
    own_meta().wait()
    lane = iota((1, 128), 1)
    own_block = lax.div(iota((8, 128), 1), 8) == iota((8, 128), 0)

    def expand(k, carry):
        values = meta_recv[k]
        bbuf[pl.ds(pl.multiple_of(k * 8, 8), 8), :] = jnp.where(
            own_block, jnp.broadcast_to(values, (8, 128)), 0.0
        )
        hot = jnp.where(lane >= 64, values, 0.0)
        xbuf[pl.ds(pl.multiple_of(k * GR, GR), GR), :] = jnp.broadcast_to(hot, (GR, 128)).astype(
            BF16
        )
        return carry

    lax.fori_loop(0, NPEER, expand, 0)
    wbuf[...] = jnp.dot(bbuf[...], across, precision=HIGHEST, preferred_element_type=F32)
    nt = (((1,), (1,)), ((), ()))
    picked = lax.dot_general(xbuf[...], spread, nt, preferred_element_type=F32)
    shape = (NPEER * GR, 256)
    same = lax.rem(iota(shape, 0), GR) == lax.rem(iota(shape, 1), GR)
    kt[...] = jnp.where(same, picked, 0.0).astype(BF16)
    placed = lax.dot_general(spread, xbuf[...], nt, preferred_element_type=F32)
    shape = (256, NPEER * GR)
    same = lax.rem(iota(shape, 0), GR) == lax.rem(iota(shape, 1), GR)
    placed = jnp.where(same, placed, 0.0).astype(BF16)
    k2[:, : NPEER * GR] = placed
    k2[:, NPEER * GR :] = placed

    def beam(k, carry):
        wide = wbuf[pl.ds(pl.multiple_of(k * 8, 8), 8), :]
        one = wide.astype(BF16).astype(F32)
        rest = wide - one
        two = rest.astype(BF16).astype(F32)
        three = rest - two
        terms = jnp.concatenate([one, two, one, three, two, one], axis=0).astype(BF16)
        field = jnp.dot(down, terms, preferred_element_type=F32)
        power = (field * field).astype(BF16)
        pbuf[:, k] = power.reshape(groups, GR, tile)
        return carry

    lax.fori_loop(0, NPEER, beam, 0)

    def add_up(product):
        step = 8
        for c in range(NPEER // step):
            values = product(c * step, (c + 1) * step).reshape(step * GR, tile)
            high = values.astype(BF16)
            low = (values - high.astype(F32)).astype(BF16)
            rhs[c * step * GR : (c + 1) * step * GR, :] = high
            rhs[(NPEER + c * step) * GR : (NPEER + (c + 1) * step) * GR, :] = low
        return jnp.dot(k2[: NT * GR, :], rhs[...], preferred_element_type=F32)

    def weights(g, carry):
        def product(a, b):
            power = pbuf[g, a:b].astype(F32)
            return power * power

        weigh[g] = add_up(product)
        return carry

    lax.fori_loop(0, groups, weights, 0)

    def swap(sums, low, high, send_sems, recv_sems):
        return (
            pltpu.make_async_remote_copy(
                src_ref=sums.at[:, pl.ds(NT * GR - SHARED, SHARED), :],
                dst_ref=low,
                send_sem=send_sems.at[0],
                recv_sem=recv_sems.at[0],
                device_id=(up, col),
                device_id_type=MESH,
            ),
            pltpu.make_async_remote_copy(
                src_ref=sums.at[:, pl.ds(0, SHARED), :],
                dst_ref=high,
                send_sem=send_sems.at[1],
                recv_sem=recv_sems.at[1],
                device_id=(below, col),
                device_id_type=MESH,
            ),
        )

    weigh_swap = swap(weigh, w_lo, w_hi, w_s, w_r)
    for copy in weigh_swap:
        copy.start()

    def sum_strip(s):
        strip = recv.at[s, pl.ds(0, NPEER - 1)]
        pltpu.make_async_copy(strip, strip, fwd_r.at[s]).wait()
        own_tile(s).wait()

        def one(g, carry):
            def product(a, b):
                return recv[s, a:b, g].astype(F32) * pbuf[s * gg + g, a:b].astype(F32)

            numer[s, g] = add_up(product)
            return carry

        lax.fori_loop(0, gg, one, 0)
        for copy in swap(numer.at[s], n_lo.at[s], n_hi.at[s], n_s.at[s], n_r.at[s]):
            copy.start()

    def joint_copies(s):
        rows = pl.ds(pl.multiple_of(side * half + s * rr, GR), rr)
        return (
            pltpu.make_async_copy(jbuf.at[s, side], joint_hbm.at[:, 0, rows, :], j_l.at[s]),
            pltpu.make_async_remote_copy(
                src_ref=jbuf.at[s, 1 - side],
                dst_ref=joint_hbm.at[:, 0, rows, :],
                send_sem=j_s.at[s],
                recv_sem=j_r.at[s],
                device_id=(row, partner),
                device_id_type=MESH,
            ),
        )

    def image_strip(s):
        for copy in swap(numer.at[s], n_lo.at[s], n_hi.at[s], n_s.at[s], n_r.at[s]):
            copy.wait_recv()

        def one(g, carry):
            at = s * gg + g
            last = NT * GR - SHARED
            ibuf[:SHARED, :] = (
                (numer[s, g, :SHARED, :] + n_lo[s, g]) / weigh[at, :SHARED, :]
            ).astype(BF16)
            ibuf[SHARED:last, :] = (numer[s, g, SHARED:last, :] / weigh[at, SHARED:last, :]).astype(
                BF16
            )
            ibuf[last:, :] = ((numer[s, g, last:, :] + n_hi[s, g]) / weigh[at, last:, :]).astype(
                BF16
            )
            for r in range(FT):
                for h in range(2):
                    first = (r * 2 + h) * GR
                    jbuf[s, h, r, pl.ds(pl.multiple_of(g * GR, GR), GR), :] = ibuf[
                        first : first + GR, :
                    ]
            step = 8
            image = ibuf[...]
            for c in range(NPEER // step):
                mine = jnp.dot(
                    kt[c * step * GR : (c + 1) * step * GR, : NT * GR],
                    image,
                    preferred_element_type=F32,
                ).reshape(step, GR, tile)
                some = pl.ds(c * step, step)
                left = recv[s, some, g].astype(F32) - pbuf[at, some].astype(F32) * mine
                ret_send[s, some, g] = left.astype(BF16)
            return carry

        lax.fori_loop(0, gg, one, 0)

        def back(i, carry):
            to = peer(i)
            pltpu.make_async_remote_copy(
                src_ref=ret_send.at[s, to],
                dst_ref=ret_recv.at[col, s],
                send_sem=ret_s.at[s],
                recv_sem=ret_r.at[s],
                device_id=(row, to),
                device_id_type=MESH,
            ).start()
            return carry

        lax.fori_loop(0, NPEER - 1, back, 0)
        own_residual(s).start()
        for copy in joint_copies(s):
            copy.start()

    def finish_weights():
        for copy in weigh_swap:
            copy.wait()
        last = NT * GR - SHARED

        def one(g, carry):
            weigh[g, :SHARED, :] = jnp.maximum(weigh[g, :SHARED, :] + w_lo[g], FLOOR)
            weigh[g, SHARED:last, :] = jnp.maximum(weigh[g, SHARED:last, :], FLOOR)
            weigh[g, last:, :] = jnp.maximum(weigh[g, last:, :] + w_hi[g], FLOOR)
            return carry

        lax.fori_loop(0, groups, one, 0)

    sum_strip(0)
    finish_weights()

    for s in range(1, strips):
        sum_strip(s)
        image_strip(s - 1)
    image_strip(strips - 1)

    sent = meta_recv.at[pl.ds(0, NPEER - 1)]
    pltpu.make_async_copy(sent, sent, meta_s).wait()

    def drain(s, carry):
        sent = recv.at[s, pl.ds(0, NPEER - 1)]
        pltpu.make_async_copy(sent, sent, fwd_s.at[s]).wait()
        sent = ret_send.at[s, pl.ds(0, NPEER - 1)]
        pltpu.make_async_copy(sent, sent, ret_s.at[s]).wait()
        pltpu.make_async_copy(sent, sent, ret_r.at[s]).wait()
        own_residual(s).wait()
        for copy in swap(numer.at[s], n_lo.at[s], n_hi.at[s], n_s.at[s], n_r.at[s]):
            copy.wait_send()
        for copy in joint_copies(s):
            copy.wait()
        return carry

    lax.fori_loop(0, strips, drain, 0)


def gather_kernel(off_ref, coef_ref, to_local_ref, d_hbm, send, meta, held, in_sem, out_sem):
    tile = held.shape[2]
    half = tile // 2
    row = lax.axis_index("row")
    top = off_ref[0, 0]
    start = lax.rem(off_ref[0, 1] + FT * top, NPEER)

    def arrive(q, h):
        t = lax.rem(q - start + NPEER, RES)
        first = pl.multiple_of(lax.div(t, FT) * tile + h * half, GR)
        across = pl.multiple_of(lax.rem(t, FT) * tile, tile)
        to = h * RES + q
        return pltpu.make_async_copy(
            d_hbm.at[0, pl.ds(first, half), pl.ds(across, tile)], held.at[to], in_sem.at[to]
        )

    def leave(to):
        return pltpu.make_async_copy(held.at[to], send.at[to], out_sem.at[to])

    for q in range(RES):
        for h in range(2):
            arrive(q, h).start()
    flat = jnp.dot(
        coef_ref[...].astype(F32), to_local_ref[...], precision=HIGHEST, preferred_element_type=F32
    )
    lane = iota((1, 128), 1)
    for t in range(RES):
        place = lax.rem(start + t, NPEER)
        target = (top - FT * row + t // FT) * 2 + lax.div(place, RES)
        meta[lax.rem(place, RES)] = jnp.where(
            lane == 64 + target, 1.0, flat[:, t * 128 : (t + 1) * 128]
        )
    for q in range(RES):
        for h in range(2):
            arrive(q, h).wait()
            leave(h * RES + q).start()
    for to in range(NPEER):
        leave(to).wait()


def place_kernel(off_ref, joint, back, joint_out, out_hbm, held, image, in_sem, out_sem, image_sem):
    tile = back.shape[2]
    half = tile // 2
    start = lax.rem(off_ref[0, 1] + FT * off_ref[0, 0], NPEER)

    def arrive(t, h):
        q = lax.rem(start + t, RES)
        rows = pl.ds((t // FT) * tile + h * half, half)
        across = pl.ds((t % FT) * tile, tile)
        return pltpu.make_async_copy(
            back.at[h * RES + q], held.at[rows, across], in_sem.at[t * 2 + h]
        )

    def leave(a, h):
        rows = pl.ds(a * tile + h * half, half)
        return pltpu.make_async_copy(held.at[rows, :], out_hbm.at[0, rows, :], out_sem.at[a * 2 + h])

    image_in = pltpu.make_async_copy(joint, image, image_sem.at[0])
    image_out = pltpu.make_async_copy(image, joint_out, image_sem.at[1])
    image_in.start()
    order = [(a, h) for a in range(FT) for h in range(2)]
    for a, h in order:
        for b in range(FT):
            arrive(a * FT + b, h).start()
    image_in.wait()
    image_out.start()
    for a, h in order:
        for b in range(FT):
            arrive(a * FT + b, h).wait()
        leave(a, h).start()
    for a, h in order:
        leave(a, h).wait()
    image_out.wait()


def local(strips, dirty, coefs, offsets):
    foot = dirty.shape[1]
    tile = foot // FT
    half = tile // 2
    rr = half // strips
    gg = rr // GR
    groups = half // GR
    vmem = pltpu.VMEM
    dma = pltpu.SemaphoreType.DMA
    tiles = (strips, NPEER, gg, GR, tile)
    by_peer = (NPEER, strips, gg, GR, tile)
    anywhere = pl.BlockSpec(memory_space=pl.ANY)
    whole = pl.BlockSpec(memory_space=pltpu.VMEM)
    scalars = pl.BlockSpec(memory_space=pltpu.SMEM)
    send, meta = pl.pallas_call(
        gather_kernel,
        out_shape=(
            jax.ShapeDtypeStruct((NPEER, half, tile), BF16),
            jax.ShapeDtypeStruct((RES, 1, 128), F32),
        ),
        in_specs=[scalars, whole, whole, anywhere],
        out_specs=(anywhere, whole),
        scratch_shapes=[vmem((NPEER, half, tile), BF16), dma((NPEER,)), dma((NPEER,))],
        compiler_params=pltpu.CompilerParams(vmem_limit_bytes=60 * 1024 * 1024),
    )(offsets, coefs, jnp.asarray(to_local_table(tile)), dirty)
    joint, back = pl.pallas_call(
        functools.partial(kernel, strips),
        out_shape=(
            jax.ShapeDtypeStruct((FT, 1, tile, tile), BF16),
            jax.ShapeDtypeStruct(by_peer, BF16),
        ),
        in_specs=[anywhere, anywhere],
        out_specs=(anywhere, anywhere),
        scratch_shapes=[
            vmem(tiles, BF16),
            vmem((groups, NPEER, GR, tile), BF16),
            vmem(tiles, BF16),
            vmem((NPEER, 1, 128), F32),
            vmem((NPEER * 8, 128), F32),
            vmem((NPEER * GR, 128), BF16),
            vmem((NPEER * 8, tile), F32),
            vmem((256, 2 * NPEER * GR), BF16),
            vmem((NPEER * GR, 256), BF16),
            vmem((2 * NPEER * GR, tile), BF16),
            vmem((groups, NT * GR, tile), F32),
            vmem((groups, SHARED, tile), F32),
            vmem((groups, SHARED, tile), F32),
            vmem((strips, gg, NT * GR, tile), F32),
            vmem((strips, gg, SHARED, tile), F32),
            vmem((strips, gg, SHARED, tile), F32),
            vmem((NT * GR, tile), BF16),
            vmem((strips, 2, FT, rr, tile), BF16),
            dma((strips,)),
            dma((strips,)),
            dma((strips,)),
            dma,
            dma,
            dma,
            dma((2,)),
            dma((2,)),
            dma((strips, 2)),
            dma((strips, 2)),
            dma((strips,)),
            dma((strips,)),
            dma((strips,)),
            dma((strips,)),
            dma((strips,)),
            dma((strips,)),
        ],
        compiler_params=pltpu.CompilerParams(
            collective_id=0, has_side_effects=True, vmem_limit_bytes=60 * 1024 * 1024
        ),
    )(send.reshape(by_peer), meta)
    return pl.pallas_call(
        place_kernel,
        out_shape=(
            jax.ShapeDtypeStruct((FT, 1, tile, tile), BF16),
            jax.ShapeDtypeStruct((1, foot, foot), BF16),
        ),
        in_specs=[scalars, anywhere, anywhere],
        out_specs=(anywhere, anywhere),
        scratch_shapes=[
            vmem((foot, foot), BF16),
            vmem((FT, 1, tile, tile), BF16),
            dma((NPEER,)),
            dma((2 * FT,)),
            dma((2,)),
        ],
        compiler_params=pltpu.CompilerParams(vmem_limit_bytes=60 * 1024 * 1024),
    )(offsets, joint, back.reshape(NPEER, half, tile))


def solution(mesh, strips=4):
    in_specs = (P(("row", "col"), None, None), P(("row", "col"), None), P(("row", "col"), None))
    out_specs = (P("row", "col", None, None), P(("row", "col"), None, None))
    return jax.shard_map(
        functools.partial(local, strips),
        mesh=mesh,
        in_specs=in_specs,
        out_specs=out_specs,
        check_vma=False,
    )
```

```python
import math

import jax
import jax.numpy as jnp
import numpy as np
from jax import lax
from jax.experimental import pallas as pl
from jax.experimental.pallas import tpu as pltpu
from jax.sharding import PartitionSpec as P

MESH = pl.DeviceIdType.MESH
FT = 4
NPEER = 32
RES = 16
ROWS7 = 7
NT = 2 * ROWS7
GR = 16
SHARED = 3 * 2 * GR
FLOOR = 0.1
AHEAD = 5
LAG = (0, 2, 4, 6, 8)
HIGHEST = lax.Precision.HIGHEST
F32 = jnp.float32
BF16 = jnp.bfloat16


def zernike_table():
    table = np.zeros((36, 8, 8))
    term = 0
    for degree in range(8):
        for azimuth in range(-degree, degree + 1, 2):
            order = abs(azimuth)
            angular = np.zeros((8, 8))
            for power in range(order + 1):
                weight = math.comb(order, power)
                if azimuth >= 0 and power % 2 == 0:
                    angular[order - power, power] += weight * (-1) ** (power // 2)
                if azimuth < 0 and power % 2 == 1:
                    angular[order - power, power] += weight * (-1) ** ((power - 1) // 2)
            for step in range((degree - order) // 2 + 1):
                radial = (
                    (-1) ** step
                    * math.factorial(degree - step)
                    / (
                        math.factorial(step)
                        * math.factorial((degree + order) // 2 - step)
                        * math.factorial((degree - order) // 2 - step)
                    )
                )
                square = (degree - 2 * step - order) // 2
                for part in range(square + 1):
                    su, sv = 2 * part, 2 * (square - part)
                    table[term, su:, sv:] += (
                        radial * math.comb(square, part) * angular[: 8 - su, : 8 - sv]
                    )
            term += 1
    return table


def to_local_table(tile):
    foot = FT * tile
    table = zernike_table()
    unit = math.sqrt(2.0) / foot
    sigma = unit * tile / 2
    shift = np.zeros((FT, 8, 8))
    for a in range(FT):
        centre = (a * tile + tile / 2 - foot / 2) * unit
        for i in range(8):
            for m in range(i + 1):
                shift[a, i, m] = math.comb(i, m) * centre ** (i - m) * sigma**m
    local = np.einsum("kij,bim,ajn->kabnm", table, shift, shift)
    to_local = np.zeros((36, RES, 128))
    to_local[:, :, :64] = local.reshape(36, RES, 64)
    return to_local.reshape(36, RES * 128).astype(np.float32)


def iota(shape, dim):
    return lax.broadcasted_iota(jnp.int32, shape, dim)


def to_power(base, exponent):
    square = base * base
    low = jnp.where(lax.rem(exponent, 2) == 1, base, 1.0)
    middle = jnp.where(lax.rem(lax.div(exponent, 2), 2) == 1, square, 1.0)
    return low * middle * jnp.where(lax.div(exponent, 4) == 1, square * square, 1.0)


def kernel(
    send,
    meta_send,
    joint_hbm,
    back,
    recv,
    beams,
    beams_all,
    ret_send,
    meta_all,
    meta_role,
    bbuf,
    xbuf,
    wbuf,
    k_all,
    k_role,
    kt,
    high,
    low,
    sums,
    from_below,
    partial,
    partial_in,
    img,
    jbuf,
    fwd_s,
    fwd_r,
    fwd_l,
    meta_s,
    meta_r,
    meta_l,
    up_s,
    up_r,
    part_s,
    part_r,
    img_s,
    img_r,
    down_s,
    down_r,
    j_s,
    j_r,
    j_l,
    ret_s,
    ret_r,
    ret_l,
):
    row = lax.axis_index("row")
    col = lax.axis_index("col")
    n_row = lax.axis_size("row")
    strips = recv.shape[0]
    tile = recv.shape[-1]
    half = tile // 2
    nx, nz = NPEER // 8, 8
    px, pz = lax.div(col, nz), lax.rem(col, nz)
    side = lax.div(col, RES)
    up = lax.rem(row + 1, n_row)
    below = lax.rem(row + n_row - 1, n_row)
    partner = lax.rem(col + RES, NPEER)

    def at(x, dz):
        return x * nz + lax.rem(pz + dz + nz, nz)

    def peer(i):
        j = lax.div(i, nx)
        last = lax.div(j, nz - 1)
        near = lax.div(j, 2) + 1
        dz = (near + lax.rem(j, 2) * (nz - 2 * near)) * (1 - last)
        return at(lax.rem(px + gray(i + last), nx), dz)

    def gray(i):
        e = lax.rem(i, nx)
        return e + lax.div(e, 2) * (1 - 2 * lax.rem(e, 2))

    barrier = pltpu.get_barrier_semaphore()

    def greet(i, carry):
        pl.semaphore_signal(barrier, inc=1, device_id=(row, peer(i)), device_id_type=MESH)
        return carry

    lax.fori_loop(0, NPEER - 1, greet, 0)
    pl.semaphore_signal(barrier, inc=1, device_id=(up, col), device_id_type=MESH)
    pl.semaphore_signal(barrier, inc=1, device_id=(below, col), device_id_type=MESH)

    def remote(src, dst, send_sem, recv_sem, to_row, to_col):
        return pltpu.make_async_remote_copy(
            src_ref=src,
            dst_ref=dst,
            send_sem=send_sem,
            recv_sem=recv_sem,
            device_id=(to_row, to_col),
            device_id_type=MESH,
        )

    def roles(dx):
        odd = lax.rem(dx, 2)
        pair = lax.div(px, 2)
        return (
            (2, 1, 4 + px),
            (-2, -1, 24 + px),
            (3, 2, 8 + px),
            (-3, -2, 28 + px),
            (4, 3 + 2 * odd, 12 + 6 * odd + pair),
            (1, 0, px),
            (-1, 0, 20 + px),
            (0, 0, 14 + px),
        )

    def send_roles(source, target, send_sem, recv_sem, local_sem):
        def one(i, carry):
            dx = gray(i)
            x = lax.rem(px + dx, nx)
            for dz, away, slot in roles(dx):
                to, centre = at(x, away), at(x, dz)
                if isinstance(away, int) and away == 0:

                    @pl.when(dx != 0)
                    def _(centre=centre, slot=slot, to=to):
                        remote(source(centre), target(slot), send_sem, recv_sem, row, to).start()
                else:
                    remote(source(centre), target(slot), send_sem, recv_sem, row, to).start()
            return carry

        lax.fori_loop(0, nx, one, 0)
        for copy in own_copies(source, target, local_sem):
            copy.start()

    def own_copies(source, target, local_sem):
        return [
            pltpu.make_async_copy(source(at(px, dz)), target(slot), local_sem.at[n])
            for n, (dz, slot) in enumerate(((1, px), (0, 14 + px), (-1, 20 + px)))
        ]

    def strip_ends(s):
        return (lambda j: send.at[j, s]), (lambda slot: recv.at[s, slot])

    def forward(s):
        send_roles(*strip_ends(s), fwd_s.at[s], fwd_r.at[s], fwd_l.at[s])

    meta_ends = (lambda j: meta_send.at[lax.rem(j, RES)]), (lambda slot: meta_role.at[slot])

    def own_meta():
        return pltpu.make_async_copy(
            meta_send.at[lax.rem(col, RES)], meta_all.at[col], meta_l.at[3]
        )

    def send_meta(i, carry):
        to = peer(i)
        remote(
            meta_send.at[lax.rem(to, RES)], meta_all.at[col], meta_s.at[1], meta_r.at[1], row, to
        ).start()
        return carry

    pl.semaphore_wait(barrier, NPEER + 1)
    send_roles(*meta_ends, meta_s.at[0], meta_r.at[0], meta_l)
    lax.fori_loop(0, NPEER - 1, send_meta, 0)
    own_meta().start()
    ahead = min(AHEAD, strips)

    def forward_strip(s, carry):
        forward(s)
        return carry

    lax.fori_loop(0, ahead, forward_strip, 0)

    shape = (128, tile)
    spot = (iota(shape, 1).astype(F32) + (0.5 - tile / 2)) * (2.0 / tile)
    across = jnp.where(iota(shape, 0) < 64, to_power(spot, lax.rem(iota(shape, 0), 8)), 0.0)
    shape = (half, 48)
    spot = ((iota(shape, 0) + side * half).astype(F32) + (0.5 - tile / 2)) * (2.0 / tile)
    whole = to_power(spot, lax.rem(iota(shape, 1), 8))
    first = whole.astype(BF16).astype(F32)
    second = (whole - first).astype(BF16).astype(F32)
    third = whole - first - second
    part = lax.div(iota(shape, 1), 8)
    down = jnp.where(
        part == 5, third, jnp.where(jnp.logical_or(part == 2, part == 4), second, first)
    ).astype(BF16)
    shape = (256, 128)
    spread = jnp.where(iota(shape, 1) == 64 + lax.div(iota(shape, 0), GR), 1.0, 0.0).astype(BF16)

    remotes = NPEER - 3
    arrived = meta_role.at[pl.ds(0, remotes)]
    pltpu.make_async_copy(arrived, arrived, meta_r.at[0]).wait()
    for copy in own_copies(*meta_ends, meta_l):
        copy.wait()
    arrived = meta_all.at[pl.ds(0, NPEER - 1)]
    pltpu.make_async_copy(arrived, arrived, meta_r.at[1]).wait()
    own_meta().wait()
    lane = iota((1, 128), 1)
    own_block = lax.div(iota((8, 128), 1), 8) == iota((8, 128), 0)

    def expand(k, carry):
        for n, meta in enumerate((meta_role, meta_all)):
            values = meta[k]
            bbuf[n, pl.ds(pl.multiple_of(k * 8, 8), 8), :] = jnp.where(
                own_block, jnp.broadcast_to(values, (8, 128)), 0.0
            )
            hot = jnp.where(lane >= 64, values, 0.0)
            xbuf[n, pl.ds(pl.multiple_of(k * GR, GR), GR), :] = jnp.broadcast_to(
                hot, (GR, 128)
            ).astype(BF16)
        return carry

    lax.fori_loop(0, NPEER, expand, 0)
    nt = (((1,), (1,)), ((), ()))

    def same(shape):
        return lax.rem(iota(shape, 0), GR) == lax.rem(iota(shape, 1), GR)

    for n in range(2):
        wbuf[n] = jnp.dot(bbuf[n], across, precision=HIGHEST, preferred_element_type=F32)
        placed = lax.dot_general(spread, xbuf[n], nt, preferred_element_type=F32)
        placed = jnp.where(same(placed.shape), placed, 0.0)
        if n == 0:
            slot = lax.div(iota(placed.shape, 1), GR)
            before = jnp.where(slot < 14, placed, 0.0).astype(BF16)
            after = jnp.where(slot >= 18, placed, 0.0).astype(BF16)
            centre = jnp.where(jnp.logical_and(slot >= 14, slot < 18), placed, 0.0).astype(BF16)
            k_role[0] = before[:, :256]
            k_role[1] = centre[:, 128:384]
            k_role[2] = after[:, 256:]
            picked = lax.dot_general(xbuf[n], spread, nt, preferred_element_type=F32)
            kt[...] = jnp.where(same(picked.shape), picked, 0.0).astype(BF16)
        else:
            k_all[...] = placed.astype(BF16)

    def beam(k, carry):
        for n, target in enumerate((beams, beams_all)):
            wide = wbuf[n, pl.ds(pl.multiple_of(k * 8, 8), 8), :]
            one = wide.astype(BF16).astype(F32)
            rest = wide - one
            two = rest.astype(BF16).astype(F32)
            three = rest - two
            terms = jnp.concatenate([one, two, one, three, two, one], axis=0).astype(BF16)
            field = jnp.dot(down, terms, preferred_element_type=F32)
            power = (field * field).astype(BF16)
            target[:, k] = power.reshape(strips, GR, tile)
        return carry

    lax.fori_loop(0, NPEER, beam, 0)

    def split(product):
        step = 8
        for c in range(NPEER // step):
            values = product(c * step, (c + 1) * step).reshape(step * GR, tile)
            some = slice(c * step * GR, (c + 1) * step * GR)
            rounded = values.astype(BF16)
            high[some, :] = rounded
            low[some, :] = (values - rounded.astype(F32)).astype(BF16)

    def add_up(matrix, start, size):
        some = slice(start, start + size)
        return jnp.dot(matrix, high[some, :], preferred_element_type=F32) + jnp.dot(
            matrix, low[some, :], preferred_element_type=F32
        )

    last = NT * GR - SHARED
    own = 2 * FT * GR

    def up_copy(s):
        return remote(
            sums.at[s, :, pl.ds(last, SHARED), :],
            from_below.at[s],
            up_s.at[s],
            up_r.at[s],
            up,
            col,
        )

    def partial_copies(s):
        return [
            remote(
                partial.at[s, n],
                partial_in.at[s, n],
                part_s.at[s, n],
                part_r.at[s, n],
                row,
                at(px, away),
            )
            for n, away in enumerate((1, -1))
        ]

    def image_copies(s):
        return [
            remote(
                img.at[s, 1, pl.ds(0, own), :],
                img.at[s, 2 * n, pl.ds(0, own), :],
                img_s.at[s, n],
                img_r.at[s, n],
                row,
                at(px, away),
            )
            for n, away in enumerate((-1, 1))
        ]

    def down_copy(s):
        return remote(
            img.at[s, :, pl.ds(0, SHARED), :],
            img.at[s, :, pl.ds(last, SHARED), :],
            down_s.at[s],
            down_r.at[s],
            below,
            col,
        )

    def joint_copies(s):
        rows = pl.ds(pl.multiple_of(side * half + s * GR, GR), GR)
        return (
            pltpu.make_async_copy(jbuf.at[s, side], joint_hbm.at[:, 0, rows, :], j_l.at[s]),
            remote(
                jbuf.at[s, 1 - side],
                joint_hbm.at[:, 0, rows, :],
                j_s.at[s],
                j_r.at[s],
                row,
                partner,
            ),
        )

    def sum_strip(s):
        strip = recv.at[s, pl.ds(0, remotes)]
        pltpu.make_async_copy(strip, strip, fwd_r.at[s]).wait()
        for copy in own_copies(*strip_ends(s), fwd_l.at[s]):
            copy.wait()
        split(lambda a, b: recv[s, a:b].astype(F32) * beams[s, a:b].astype(F32))
        for n in range(3):
            sums[s, n] = add_up(k_role[n, : NT * GR, :], n * 128, 256)

        def squares(a, b):
            power = beams_all[s, a:b].astype(F32)
            return power * power

        split(squares)
        sums[s, 3] = add_up(k_all[: NT * GR, :], 0, NPEER * GR)
        up_copy(s).start()

    def partial_strip(s):
        up_copy(s).wait_recv()
        for n in range(2):
            partial[s, n, :SHARED, :] = (
                sums[s, 2 * n, :SHARED, :] + from_below[s, 2 * n]
            ).astype(BF16)
            partial[s, n, SHARED:, :] = sums[s, 2 * n, SHARED:own, :].astype(BF16)
        for copy in partial_copies(s):
            copy.start()

    def image_strip(s):
        for copy in partial_copies(s):
            copy.wait_recv()
        off = partial_in[s, 0].astype(F32) + partial_in[s, 1].astype(F32)
        numer = sums[s, 1, :SHARED, :] + from_below[s, 1] + off[:SHARED]
        weigh = jnp.maximum(sums[s, 3, :SHARED, :] + from_below[s, 3], FLOOR)
        img[s, 1, :SHARED, :] = (numer / weigh).astype(BF16)
        numer = sums[s, 1, SHARED:own, :] + off[SHARED:]
        weigh = jnp.maximum(sums[s, 3, SHARED:own, :], FLOOR)
        img[s, 1, SHARED:own, :] = (numer / weigh).astype(BF16)
        for copy in image_copies(s):
            copy.start()
        for r in range(FT):
            for h in range(2):
                first = (r * 2 + h) * GR
                jbuf[s, h, r] = img[s, 1, first : first + GR, :]
        for copy in joint_copies(s):
            copy.start()

    def pass_strip(s):
        for copy in image_copies(s):
            copy.wait_recv()
        down_copy(s).start()

    def own_back(s):
        return [
            pltpu.make_async_copy(
                ret_send.at[s, slot], back.at[at(px, dz), s], ret_l.at[s, n]
            )
            for n, (dz, slot) in enumerate(((1, px), (0, 14 + px), (-1, 20 + px)))
        ]

    def residual_strip(s):
        down_copy(s).wait_recv()
        for n, a, b in ((0, 0, 7), (0, 7, 14), (1, 14, 18), (2, 18, 25), (2, 25, 32)):
            mine = jnp.dot(
                kt[a * GR : b * GR, : NT * GR], img[s, n], preferred_element_type=F32
            ).reshape(b - a, GR, tile)
            left = recv[s, a:b].astype(F32) - beams[s, a:b].astype(F32) * mine
            ret_send[s, a:b] = left.astype(BF16)

        def one(i, carry):
            dx = gray(i)
            x = lax.rem(px + dx, nx)
            odd = lax.rem(dx, 2)
            ways = (
                (1, -1, 4 + x),
                (-1, 1, 24 + x),
                (1, -2, 8 + x),
                (-1, 2, 28 + x),
                (1 - 2 * odd, 5 - 2 * odd, 12 + 6 * odd + lax.div(x, 2)),
                (1, 0, x),
                (-1, 0, 20 + x),
                (0, 0, 14 + x),
            )
            for dz, away, slot in ways:

                def go(dz=dz, away=away, slot=slot):
                    remote(
                        ret_send.at[s, slot],
                        back.at[at(px, dz), s],
                        ret_s.at[s],
                        ret_r.at[s],
                        row,
                        at(x, away),
                    ).start()

                if isinstance(away, int) and away == 0:
                    pl.when(dx != 0)(go)
                else:
                    go()
            return carry

        lax.fori_loop(0, nx, one, 0)
        for copy in own_back(s):
            copy.start()

    stages = (sum_strip, partial_strip, image_strip, pass_strip, residual_strip)

    def step(i, carry):
        for n in (0, 1, 2, 3, 4):
            pl.when(jnp.logical_and(i >= LAG[n], i < strips + LAG[n]))(lambda n=n: stages[n](i - LAG[n]))
        pl.when(i + ahead < strips)(lambda: forward(i + ahead))
        return carry

    lax.fori_loop(0, strips + LAG[-1], step, 0)

    sent = meta_role.at[pl.ds(0, remotes)]
    pltpu.make_async_copy(sent, sent, meta_s.at[0]).wait()
    sent = meta_all.at[pl.ds(0, NPEER - 1)]
    pltpu.make_async_copy(sent, sent, meta_s.at[1]).wait()

    def drain(s, carry):
        sent = recv.at[s, pl.ds(0, remotes)]
        pltpu.make_async_copy(sent, sent, fwd_s.at[s]).wait()
        up_copy(s).wait_send()
        for copy in partial_copies(s):
            copy.wait_send()
        for copy in image_copies(s):
            copy.wait_send()
        down_copy(s).wait_send()
        for copy in joint_copies(s):
            copy.wait()
        sent = ret_send.at[s, pl.ds(0, remotes)]
        pltpu.make_async_copy(sent, sent, ret_s.at[s]).wait()
        pltpu.make_async_copy(sent, sent, ret_r.at[s]).wait()
        for copy in own_back(s):
            copy.wait()
        return carry

    lax.fori_loop(0, strips, drain, 0)


def gather_kernel(off_ref, coef_ref, to_local_ref, d_hbm, send, meta, held, in_sem, out_sem):
    tile = held.shape[2]
    half = tile // 2
    row = lax.axis_index("row")
    top = off_ref[0, 0]
    start = lax.rem(off_ref[0, 1] + FT * top, NPEER)

    def arrive(q, h):
        t = lax.rem(q - start + NPEER, RES)
        first = pl.multiple_of(lax.div(t, FT) * tile + h * half, GR)
        across = pl.multiple_of(lax.rem(t, FT) * tile, tile)
        to = h * RES + q
        return pltpu.make_async_copy(
            d_hbm.at[0, pl.ds(first, half), pl.ds(across, tile)], held.at[to], in_sem.at[to]
        )

    def leave(to):
        return pltpu.make_async_copy(held.at[to], send.at[to], out_sem.at[to])

    for q in range(RES):
        for h in range(2):
            arrive(q, h).start()
    flat = jnp.dot(
        coef_ref[...].astype(F32), to_local_ref[...], precision=HIGHEST, preferred_element_type=F32
    )
    lane = iota((1, 128), 1)
    for t in range(RES):
        place = lax.rem(start + t, NPEER)
        target = (top - FT * row + t // FT) * 2 + lax.div(place, RES)
        meta[lax.rem(place, RES)] = jnp.where(
            lane == 64 + target, 1.0, flat[:, t * 128 : (t + 1) * 128]
        )
    for q in range(RES):
        for h in range(2):
            arrive(q, h).wait()
            leave(h * RES + q).start()
    for to in range(NPEER):
        leave(to).wait()


def place_kernel(off_ref, joint, back, joint_out, out_hbm, held, image, in_sem, out_sem, image_sem):
    tile = back.shape[2]
    half = tile // 2
    start = lax.rem(off_ref[0, 1] + FT * off_ref[0, 0], NPEER)

    def arrive(t, h):
        q = lax.rem(start + t, RES)
        rows = pl.ds((t // FT) * tile + h * half, half)
        across = pl.ds((t % FT) * tile, tile)
        return pltpu.make_async_copy(
            back.at[h * RES + q], held.at[rows, across], in_sem.at[t * 2 + h]
        )

    def leave(a, h):
        rows = pl.ds(a * tile + h * half, half)
        return pltpu.make_async_copy(held.at[rows, :], out_hbm.at[0, rows, :], out_sem.at[a * 2 + h])

    image_in = pltpu.make_async_copy(joint, image, image_sem.at[0])
    image_out = pltpu.make_async_copy(image, joint_out, image_sem.at[1])
    image_in.start()
    order = [(a, h) for a in range(FT) for h in range(2)]
    for a, h in order:
        for b in range(FT):
            arrive(a * FT + b, h).start()
    image_in.wait()
    image_out.start()
    for a, h in order:
        for b in range(FT):
            arrive(a * FT + b, h).wait()
        leave(a, h).start()
    for a, h in order:
        leave(a, h).wait()
    image_out.wait()


def local(dirty, coefs, offsets):
    foot = dirty.shape[1]
    tile = foot // FT
    half = tile // 2
    strips = half // GR
    vmem = pltpu.VMEM
    dma = pltpu.SemaphoreType.DMA
    tiles = (strips, NPEER, GR, tile)
    by_peer = (NPEER, strips, GR, tile)
    anywhere = pl.BlockSpec(memory_space=pl.ANY)
    whole = pl.BlockSpec(memory_space=pltpu.VMEM)
    scalars = pl.BlockSpec(memory_space=pltpu.SMEM)
    send, meta = pl.pallas_call(
        gather_kernel,
        out_shape=(
            jax.ShapeDtypeStruct((NPEER, half, tile), BF16),
            jax.ShapeDtypeStruct((RES, 1, 128), F32),
        ),
        in_specs=[scalars, whole, whole, anywhere],
        out_specs=(anywhere, whole),
        scratch_shapes=[vmem((NPEER, half, tile), BF16), dma((NPEER,)), dma((NPEER,))],
        compiler_params=pltpu.CompilerParams(vmem_limit_bytes=60 * 1024 * 1024),
    )(offsets, coefs, jnp.asarray(to_local_table(tile)), dirty)
    joint, back = pl.pallas_call(
        kernel,
        out_shape=(
            jax.ShapeDtypeStruct((FT, 1, tile, tile), BF16),
            jax.ShapeDtypeStruct(by_peer, BF16),
        ),
        in_specs=[anywhere, anywhere],
        out_specs=(anywhere, anywhere),
        scratch_shapes=[
            vmem(tiles, BF16),
            vmem(tiles, BF16),
            vmem(tiles, BF16),
            vmem(tiles, BF16),
            vmem((NPEER, 1, 128), F32),
            vmem((NPEER, 1, 128), F32),
            vmem((2, NPEER * 8, 128), F32),
            vmem((2, NPEER * GR, 128), BF16),
            vmem((2, NPEER * 8, tile), F32),
            vmem((256, NPEER * GR), BF16),
            vmem((3, 256, 256), BF16),
            vmem((NPEER * GR, 256), BF16),
            vmem((NPEER * GR, tile), BF16),
            vmem((NPEER * GR, tile), BF16),
            vmem((strips, 4, NT * GR, tile), F32),
            vmem((strips, 4, SHARED, tile), F32),
            vmem((strips, 2, 2 * FT * GR, tile), BF16),
            vmem((strips, 2, 2 * FT * GR, tile), BF16),
            vmem((strips, 3, NT * GR, tile), BF16),
            vmem((strips, 2, FT, GR, tile), BF16),
            dma((strips,)),
            dma((strips,)),
            dma((strips, 3)),
            dma((2,)),
            dma((2,)),
            dma((4,)),
            dma((strips,)),
            dma((strips,)),
            dma((strips, 2)),
            dma((strips, 2)),
            dma((strips, 2)),
            dma((strips, 2)),
            dma((strips,)),
            dma((strips,)),
            dma((strips,)),
            dma((strips,)),
            dma((strips,)),
            dma((strips,)),
            dma((strips,)),
            dma((strips, 3)),
        ],
        compiler_params=pltpu.CompilerParams(
            collective_id=0, has_side_effects=True, vmem_limit_bytes=60 * 1024 * 1024
        ),
    )(send.reshape(by_peer), meta)
    return pl.pallas_call(
        place_kernel,
        out_shape=(
            jax.ShapeDtypeStruct((FT, 1, tile, tile), BF16),
            jax.ShapeDtypeStruct((1, foot, foot), BF16),
        ),
        in_specs=[scalars, anywhere, anywhere],
        out_specs=(anywhere, anywhere),
        scratch_shapes=[
            vmem((foot, foot), BF16),
            vmem((FT, 1, tile, tile), BF16),
            dma((NPEER,)),
            dma((2 * FT,)),
            dma((2,)),
        ],
        compiler_params=pltpu.CompilerParams(vmem_limit_bytes=60 * 1024 * 1024),
    )(offsets, joint, back.reshape(NPEER, half, tile))


def solution(mesh):
    in_specs = (P(("row", "col"), None, None), P(("row", "col"), None), P(("row", "col"), None))
    out_specs = (P("row", "col", None, None), P(("row", "col"), None, None))
    return jax.shard_map(
        local, mesh=mesh, in_specs=in_specs, out_specs=out_specs, check_vma=False
    )
```

```python
import functools
import math

import jax
import jax.numpy as jnp
import numpy as np
from jax import lax
from jax.experimental import pallas as pl
from jax.experimental.pallas import tpu as pltpu
from jax.sharding import PartitionSpec as P

MESH = pl.DeviceIdType.MESH
FT = 4
NPEER = 32
RES = 16
ROWS7 = 7
NT = 2 * ROWS7
GR = 16
SHARED = 3 * 2 * GR
FLOOR = 0.1
AHEAD = 5
MAIN_VMEM = 44 * 1024 * 1024
SMALL_VMEM = 16 * 1024 * 1024
LAG = (0, 2, 4, 6, 8)
HIGHEST = lax.Precision.HIGHEST
F32 = jnp.float32
BF16 = jnp.bfloat16


def zernike_table():
    table = np.zeros((36, 8, 8))
    term = 0
    for degree in range(8):
        for azimuth in range(-degree, degree + 1, 2):
            order = abs(azimuth)
            angular = np.zeros((8, 8))
            for power in range(order + 1):
                weight = math.comb(order, power)
                if azimuth >= 0 and power % 2 == 0:
                    angular[order - power, power] += weight * (-1) ** (power // 2)
                if azimuth < 0 and power % 2 == 1:
                    angular[order - power, power] += weight * (-1) ** ((power - 1) // 2)
            for step in range((degree - order) // 2 + 1):
                radial = (
                    (-1) ** step
                    * math.factorial(degree - step)
                    / (
                        math.factorial(step)
                        * math.factorial((degree + order) // 2 - step)
                        * math.factorial((degree - order) // 2 - step)
                    )
                )
                square = (degree - 2 * step - order) // 2
                for part in range(square + 1):
                    su, sv = 2 * part, 2 * (square - part)
                    table[term, su:, sv:] += (
                        radial * math.comb(square, part) * angular[: 8 - su, : 8 - sv]
                    )
            term += 1
    return table


def to_local_table(tile):
    foot = FT * tile
    table = zernike_table()
    unit = math.sqrt(2.0) / foot
    sigma = unit * tile / 2
    shift = np.zeros((FT, 8, 8))
    for a in range(FT):
        centre = (a * tile + tile / 2 - foot / 2) * unit
        for i in range(8):
            for m in range(i + 1):
                shift[a, i, m] = math.comb(i, m) * centre ** (i - m) * sigma**m
    local = np.einsum("kij,bim,ajn->kabnm", table, shift, shift)
    to_local = np.zeros((36, RES, 128))
    to_local[:, :, :64] = local.reshape(36, RES, 64)
    return to_local.reshape(36, RES * 128).astype(np.float32)


def iota(shape, dim):
    return lax.broadcasted_iota(jnp.int32, shape, dim)


def to_power(base, exponent):
    square = base * base
    low = jnp.where(lax.rem(exponent, 2) == 1, base, 1.0)
    middle = jnp.where(lax.rem(lax.div(exponent, 2), 2) == 1, square, 1.0)
    return low * middle * jnp.where(lax.div(exponent, 4) == 1, square * square, 1.0)


def kernel(
    send,
    meta_send,
    joint_hbm,
    back,
    recv,
    beams,
    beams_all,
    ret_send,
    meta_all,
    meta_role,
    bbuf,
    xbuf,
    wbuf,
    k_all,
    k_role,
    kt,
    high,
    low,
    sums,
    from_below,
    partial,
    partial_in,
    img,
    jbuf,
    fwd_s,
    fwd_r,
    fwd_l,
    meta_s,
    meta_r,
    meta_l,
    up_s,
    up_r,
    part_s,
    part_r,
    img_s,
    img_r,
    down_s,
    down_r,
    j_s,
    j_r,
    j_l,
    ret_s,
    ret_r,
    ret_l,
):
    row = lax.axis_index("row")
    col = lax.axis_index("col")
    n_row = lax.axis_size("row")
    strips = recv.shape[0]
    tile = recv.shape[-1]
    half = tile // 2
    nx, nz = NPEER // 8, 8
    px, pz = lax.div(col, nz), lax.rem(col, nz)
    side = lax.div(col, RES)
    up = lax.rem(row + 1, n_row)
    below = lax.rem(row + n_row - 1, n_row)
    partner = lax.rem(col + RES, NPEER)

    def at(x, dz):
        return x * nz + lax.rem(pz + dz + nz, nz)

    def peer(i):
        j = lax.div(i, nx)
        last = lax.div(j, nz - 1)
        near = lax.div(j, 2) + 1
        dz = (near + lax.rem(j, 2) * (nz - 2 * near)) * (1 - last)
        return at(lax.rem(px + gray(i + last), nx), dz)

    def gray(i):
        e = lax.rem(i, nx)
        return e + lax.div(e, 2) * (1 - 2 * lax.rem(e, 2))

    barrier = pltpu.get_barrier_semaphore()

    def greet(i, carry):
        pl.semaphore_signal(barrier, inc=1, device_id=(row, peer(i)), device_id_type=MESH)
        return carry

    lax.fori_loop(0, NPEER - 1, greet, 0)
    pl.semaphore_signal(barrier, inc=1, device_id=(up, col), device_id_type=MESH)
    pl.semaphore_signal(barrier, inc=1, device_id=(below, col), device_id_type=MESH)

    def remote(src, dst, send_sem, recv_sem, to_row, to_col):
        return pltpu.make_async_remote_copy(
            src_ref=src,
            dst_ref=dst,
            send_sem=send_sem,
            recv_sem=recv_sem,
            device_id=(to_row, to_col),
            device_id_type=MESH,
        )

    def roles(dx):
        odd = lax.rem(dx, 2)
        pair = lax.div(px, 2)
        return (
            (2, 1, 4 + px),
            (-2, -1, 24 + px),
            (3, 2, 8 + px),
            (-3, -2, 28 + px),
            (4, 3 + 2 * odd, 12 + 6 * odd + pair),
            (1, 0, px),
            (-1, 0, 20 + px),
            (0, 0, 14 + px),
        )

    def send_roles(source, target, send_sem, recv_sem, local_sem):
        def one(i, carry):
            dx = gray(i)
            x = lax.rem(px + dx, nx)
            for dz, away, slot in roles(dx):
                to, centre = at(x, away), at(x, dz)
                if isinstance(away, int) and away == 0:

                    @pl.when(dx != 0)
                    def _(centre=centre, slot=slot, to=to):
                        remote(source(centre), target(slot), send_sem, recv_sem, row, to).start()
                else:
                    remote(source(centre), target(slot), send_sem, recv_sem, row, to).start()
            return carry

        lax.fori_loop(0, nx, one, 0)
        for copy in own_copies(source, target, local_sem):
            copy.start()

    def own_copies(source, target, local_sem):
        return [
            pltpu.make_async_copy(source(at(px, dz)), target(slot), local_sem.at[n])
            for n, (dz, slot) in enumerate(((1, px), (0, 14 + px), (-1, 20 + px)))
        ]

    def strip_ends(s):
        return (lambda j: send.at[j, s]), (lambda slot: recv.at[s, slot])

    def forward(s):
        send_roles(*strip_ends(s), fwd_s.at[s], fwd_r.at[s], fwd_l.at[s])

    meta_ends = (lambda j: meta_send.at[lax.rem(j, RES)]), (lambda slot: meta_role.at[slot])

    def own_meta():
        return pltpu.make_async_copy(
            meta_send.at[lax.rem(col, RES)], meta_all.at[col], meta_l.at[3]
        )

    def send_meta(i, carry):
        to = peer(i)
        remote(
            meta_send.at[lax.rem(to, RES)], meta_all.at[col], meta_s.at[1], meta_r.at[1], row, to
        ).start()
        return carry

    pl.semaphore_wait(barrier, NPEER + 1)
    send_roles(*meta_ends, meta_s.at[0], meta_r.at[0], meta_l)
    lax.fori_loop(0, NPEER - 1, send_meta, 0)
    own_meta().start()
    ahead = min(AHEAD, strips)

    def forward_strip(s, carry):
        forward(s)
        return carry

    lax.fori_loop(0, ahead, forward_strip, 0)

    shape = (128, tile)
    spot = (iota(shape, 1).astype(F32) + (0.5 - tile / 2)) * (2.0 / tile)
    across = jnp.where(iota(shape, 0) < 64, to_power(spot, lax.rem(iota(shape, 0), 8)), 0.0)
    shape = (half, 48)
    spot = ((iota(shape, 0) + side * half).astype(F32) + (0.5 - tile / 2)) * (2.0 / tile)
    whole = to_power(spot, lax.rem(iota(shape, 1), 8))
    first = whole.astype(BF16).astype(F32)
    second = (whole - first).astype(BF16).astype(F32)
    third = whole - first - second
    part = lax.div(iota(shape, 1), 8)
    down = jnp.where(
        part == 5, third, jnp.where(jnp.logical_or(part == 2, part == 4), second, first)
    ).astype(BF16)
    shape = (256, 128)
    spread = jnp.where(iota(shape, 1) == 64 + lax.div(iota(shape, 0), GR), 1.0, 0.0).astype(BF16)

    remotes = NPEER - 3
    arrived = meta_role.at[pl.ds(0, remotes)]
    pltpu.make_async_copy(arrived, arrived, meta_r.at[0]).wait()
    for copy in own_copies(*meta_ends, meta_l):
        copy.wait()
    arrived = meta_all.at[pl.ds(0, NPEER - 1)]
    pltpu.make_async_copy(arrived, arrived, meta_r.at[1]).wait()
    own_meta().wait()
    lane = iota((1, 128), 1)
    own_block = lax.div(iota((8, 128), 1), 8) == iota((8, 128), 0)

    def expand(k, carry):
        for n, meta in enumerate((meta_role, meta_all)):
            values = meta[k]
            bbuf[n, pl.ds(pl.multiple_of(k * 8, 8), 8), :] = jnp.where(
                own_block, jnp.broadcast_to(values, (8, 128)), 0.0
            )
            hot = jnp.where(lane >= 64, values, 0.0)
            xbuf[n, pl.ds(pl.multiple_of(k * GR, GR), GR), :] = jnp.broadcast_to(
                hot, (GR, 128)
            ).astype(BF16)
        return carry

    lax.fori_loop(0, NPEER, expand, 0)
    nt = (((1,), (1,)), ((), ()))

    def same(shape):
        return lax.rem(iota(shape, 0), GR) == lax.rem(iota(shape, 1), GR)

    for n in range(2):
        wbuf[n] = jnp.dot(bbuf[n], across, precision=HIGHEST, preferred_element_type=F32)
        placed = lax.dot_general(spread, xbuf[n], nt, preferred_element_type=F32)
        placed = jnp.where(same(placed.shape), placed, 0.0)
        if n == 0:
            slot = lax.div(iota(placed.shape, 1), GR)
            before = jnp.where(slot < 14, placed, 0.0).astype(BF16)
            after = jnp.where(slot >= 18, placed, 0.0).astype(BF16)
            centre = jnp.where(jnp.logical_and(slot >= 14, slot < 18), placed, 0.0).astype(BF16)
            k_role[0] = before[:, :256]
            k_role[1] = centre[:, 128:384]
            k_role[2] = after[:, 256:]
            picked = lax.dot_general(xbuf[n], spread, nt, preferred_element_type=F32)
            kt[...] = jnp.where(same(picked.shape), picked, 0.0).astype(BF16)
        else:
            k_all[...] = placed.astype(BF16)

    def beam(k, carry):
        for n, target in enumerate((beams, beams_all)):
            wide = wbuf[n, pl.ds(pl.multiple_of(k * 8, 8), 8), :]
            one = wide.astype(BF16).astype(F32)
            rest = wide - one
            two = rest.astype(BF16).astype(F32)
            three = rest - two
            terms = jnp.concatenate([one, two, one, three, two, one], axis=0).astype(BF16)
            field = jnp.dot(down, terms, preferred_element_type=F32)
            power = (field * field).astype(BF16)
            target[:, k] = power.reshape(strips, GR, tile)
        return carry

    lax.fori_loop(0, NPEER, beam, 0)

    def split(product):
        step = 8
        for c in range(NPEER // step):
            values = product(c * step, (c + 1) * step).reshape(step * GR, tile)
            some = slice(c * step * GR, (c + 1) * step * GR)
            rounded = values.astype(BF16)
            high[some, :] = rounded
            low[some, :] = (values - rounded.astype(F32)).astype(BF16)

    def add_up(matrix, start, size):
        some = slice(start, start + size)
        return jnp.dot(matrix, high[some, :], preferred_element_type=F32) + jnp.dot(
            matrix, low[some, :], preferred_element_type=F32
        )

    last = NT * GR - SHARED
    own = 2 * FT * GR

    def up_copy(s):
        return remote(
            sums.at[s, :, pl.ds(last, SHARED), :],
            from_below.at[s],
            up_s.at[s],
            up_r.at[s],
            up,
            col,
        )

    def partial_copies(s):
        return [
            remote(
                partial.at[s, n],
                partial_in.at[s, n],
                part_s.at[s, n],
                part_r.at[s, n],
                row,
                at(px, away),
            )
            for n, away in enumerate((1, -1))
        ]

    def image_copies(s):
        return [
            remote(
                img.at[s, 1, pl.ds(0, own), :],
                img.at[s, 2 * n, pl.ds(0, own), :],
                img_s.at[s, n],
                img_r.at[s, n],
                row,
                at(px, away),
            )
            for n, away in enumerate((-1, 1))
        ]

    def down_copy(s):
        return remote(
            img.at[s, :, pl.ds(0, SHARED), :],
            img.at[s, :, pl.ds(last, SHARED), :],
            down_s.at[s],
            down_r.at[s],
            below,
            col,
        )

    def joint_copies(s):
        rows = pl.ds(pl.multiple_of(side * half + s * GR, GR), GR)
        return (
            pltpu.make_async_copy(jbuf.at[s, side], joint_hbm.at[:, 0, rows, :], j_l.at[s]),
            remote(
                jbuf.at[s, 1 - side],
                joint_hbm.at[:, 0, rows, :],
                j_s.at[s],
                j_r.at[s],
                row,
                partner,
            ),
        )

    def sum_strip(s):
        strip = recv.at[s, pl.ds(0, remotes)]
        pltpu.make_async_copy(strip, strip, fwd_r.at[s]).wait()
        for copy in own_copies(*strip_ends(s), fwd_l.at[s]):
            copy.wait()
        split(lambda a, b: recv[s, a:b].astype(F32) * beams[s, a:b].astype(F32))
        for n in range(3):
            sums[s, n] = add_up(k_role[n, : NT * GR, :], n * 128, 256)

        def squares(a, b):
            power = beams_all[s, a:b].astype(F32)
            return power * power

        split(squares)
        sums[s, 3] = add_up(k_all[: NT * GR, :], 0, NPEER * GR)
        up_copy(s).start()

    def partial_strip(s):
        up_copy(s).wait_recv()
        for n in range(2):
            partial[s, n, :SHARED, :] = (
                sums[s, 2 * n, :SHARED, :] + from_below[s, 2 * n]
            ).astype(BF16)
            partial[s, n, SHARED:, :] = sums[s, 2 * n, SHARED:own, :].astype(BF16)
        for copy in partial_copies(s):
            copy.start()

    def image_strip(s):
        for copy in partial_copies(s):
            copy.wait_recv()
        off = partial_in[s, 0].astype(F32) + partial_in[s, 1].astype(F32)
        numer = sums[s, 1, :SHARED, :] + from_below[s, 1] + off[:SHARED]
        weigh = jnp.maximum(sums[s, 3, :SHARED, :] + from_below[s, 3], FLOOR)
        img[s, 1, :SHARED, :] = (numer / weigh).astype(BF16)
        numer = sums[s, 1, SHARED:own, :] + off[SHARED:]
        weigh = jnp.maximum(sums[s, 3, SHARED:own, :], FLOOR)
        img[s, 1, SHARED:own, :] = (numer / weigh).astype(BF16)
        for copy in image_copies(s):
            copy.start()
        for r in range(FT):
            for h in range(2):
                first = (r * 2 + h) * GR
                jbuf[s, h, r] = img[s, 1, first : first + GR, :]
        for copy in joint_copies(s):
            copy.start()

    def pass_strip(s):
        for copy in image_copies(s):
            copy.wait_recv()
        down_copy(s).start()

    def own_back(s):
        return [
            pltpu.make_async_copy(
                ret_send.at[s, slot], back.at[at(px, dz), s], ret_l.at[s, n]
            )
            for n, (dz, slot) in enumerate(((1, px), (0, 14 + px), (-1, 20 + px)))
        ]

    def residual_strip(s):
        down_copy(s).wait_recv()
        for n, a, b in ((0, 0, 7), (0, 7, 14), (1, 14, 18), (2, 18, 25), (2, 25, 32)):
            mine = jnp.dot(
                kt[a * GR : b * GR, : NT * GR], img[s, n], preferred_element_type=F32
            ).reshape(b - a, GR, tile)
            left = recv[s, a:b].astype(F32) - beams[s, a:b].astype(F32) * mine
            ret_send[s, a:b] = left.astype(BF16)

        def one(i, carry):
            dx = gray(i)
            x = lax.rem(px + dx, nx)
            odd = lax.rem(dx, 2)
            ways = (
                (1, -1, 4 + x),
                (-1, 1, 24 + x),
                (1, -2, 8 + x),
                (-1, 2, 28 + x),
                (1 - 2 * odd, 5 - 2 * odd, 12 + 6 * odd + lax.div(x, 2)),
                (1, 0, x),
                (-1, 0, 20 + x),
                (0, 0, 14 + x),
            )
            for dz, away, slot in ways:

                def go(dz=dz, away=away, slot=slot):
                    remote(
                        ret_send.at[s, slot],
                        back.at[at(px, dz), s],
                        ret_s.at[s],
                        ret_r.at[s],
                        row,
                        at(x, away),
                    ).start()

                if isinstance(away, int) and away == 0:
                    pl.when(dx != 0)(go)
                else:
                    go()
            return carry

        lax.fori_loop(0, nx, one, 0)
        for copy in own_back(s):
            copy.start()

    stages = (sum_strip, partial_strip, image_strip, pass_strip, residual_strip)

    def step(i, carry):
        for n in (0, 1, 2, 3, 4):
            pl.when(jnp.logical_and(i >= LAG[n], i < strips + LAG[n]))(lambda n=n: stages[n](i - LAG[n]))
        pl.when(i + ahead < strips)(lambda: forward(i + ahead))
        return carry

    lax.fori_loop(0, strips + LAG[-1], step, 0)

    sent = meta_role.at[pl.ds(0, remotes)]
    pltpu.make_async_copy(sent, sent, meta_s.at[0]).wait()
    sent = meta_all.at[pl.ds(0, NPEER - 1)]
    pltpu.make_async_copy(sent, sent, meta_s.at[1]).wait()

    def drain(s, carry):
        sent = recv.at[s, pl.ds(0, remotes)]
        pltpu.make_async_copy(sent, sent, fwd_s.at[s]).wait()
        up_copy(s).wait_send()
        for copy in partial_copies(s):
            copy.wait_send()
        for copy in image_copies(s):
            copy.wait_send()
        down_copy(s).wait_send()
        for copy in joint_copies(s):
            copy.wait()
        sent = ret_send.at[s, pl.ds(0, remotes)]
        pltpu.make_async_copy(sent, sent, ret_s.at[s]).wait()
        pltpu.make_async_copy(sent, sent, ret_r.at[s]).wait()
        for copy in own_back(s):
            copy.wait()
        return carry

    lax.fori_loop(0, strips, drain, 0)


def gather_kernel(off_ref, coef_ref, to_local_ref, d_hbm, send, meta, sem):
    strips, tile = send.shape[1], send.shape[3]
    row = lax.axis_index("row")
    top = off_ref[0, 0]
    start = lax.rem(off_ref[0, 1] + FT * top, NPEER)

    def move(q, h):
        t = lax.rem(q - start + NPEER, RES)
        first = (lax.div(t, FT) * 2 + h) * strips
        across = pl.multiple_of(lax.rem(t, FT) * tile, tile)
        to = h * RES + q
        return pltpu.make_async_copy(
            d_hbm.at[pl.ds(first, strips), :, pl.ds(across, tile)], send.at[to], sem.at[to]
        )

    moves = [move(q, h) for q in range(RES) for h in range(2)]
    for copy in moves:
        copy.start()
    flat = jnp.dot(
        coef_ref[...].astype(F32), to_local_ref[...], precision=HIGHEST, preferred_element_type=F32
    )
    lane = iota((1, 128), 1)
    for t in range(RES):
        place = lax.rem(start + t, NPEER)
        target = (top - FT * row + t // FT) * 2 + lax.div(place, RES)
        meta[lax.rem(place, RES)] = jnp.where(
            lane == 64 + target, 1.0, flat[:, t * 128 : (t + 1) * 128]
        )
    for copy in moves:
        copy.wait()


def place_kernel(off_ref, joint, back, joint_out, out_hbm, sem):
    strips, tile = back.shape[1], back.shape[3]
    start = lax.rem(off_ref[0, 1] + FT * off_ref[0, 0], NPEER)

    def move(t, h):
        q = lax.rem(start + t, RES)
        rows = pl.ds(((t // FT) * 2 + h) * strips, strips)
        across = pl.ds((t % FT) * tile, tile)
        return pltpu.make_async_copy(
            back.at[h * RES + q], out_hbm.at[rows, :, across], sem.at[t * 2 + h]
        )

    moves = [move(t, h) for t in range(RES) for h in range(2)]
    moves.append(pltpu.make_async_copy(joint, joint_out, sem.at[NPEER]))
    for copy in moves:
        copy.start()
    for copy in moves:
        copy.wait()


def local(dirty, coefs, offsets):
    foot = dirty.shape[1]
    tile = foot // FT
    half = tile // 2
    strips = half // GR
    vmem = pltpu.VMEM
    dma = pltpu.SemaphoreType.DMA
    tiles = (strips, NPEER, GR, tile)
    by_peer = (NPEER, strips, GR, tile)
    footprint = (foot // GR, GR, foot)
    image = (FT, 1, tile, tile)
    anywhere = pl.BlockSpec(memory_space=pl.ANY)
    whole = pl.BlockSpec(memory_space=pltpu.VMEM)
    scalars = pl.BlockSpec(memory_space=pltpu.SMEM)
    in_hbm = functools.partial(pltpu.with_memory_space_constraint, memory_space=pltpu.HBM)
    in_vmem = functools.partial(pltpu.with_memory_space_constraint, memory_space=pltpu.VMEM)
    offsets = in_hbm(offsets)
    send, meta = pl.pallas_call(
        gather_kernel,
        out_shape=(pltpu.VMEM(by_peer, BF16), pltpu.VMEM((RES, 1, 128), F32)),
        in_specs=[scalars, whole, whole, anywhere],
        out_specs=(anywhere, whole),
        scratch_shapes=[dma((NPEER,))],
        compiler_params=pltpu.CompilerParams(vmem_limit_bytes=SMALL_VMEM),
    )(
        offsets,
        in_hbm(coefs),
        in_hbm(jnp.asarray(to_local_table(tile))),
        in_hbm(dirty.reshape(footprint)),
    )
    joint, back = pl.pallas_call(
        kernel,
        out_shape=(pltpu.VMEM(image, BF16), pltpu.VMEM(by_peer, BF16)),
        in_specs=[anywhere, anywhere],
        out_specs=(anywhere, anywhere),
        scratch_shapes=[
            vmem(tiles, BF16),
            vmem(tiles, BF16),
            vmem(tiles, BF16),
            vmem(tiles, BF16),
            vmem((NPEER, 1, 128), F32),
            vmem((NPEER, 1, 128), F32),
            vmem((2, NPEER * 8, 128), F32),
            vmem((2, NPEER * GR, 128), BF16),
            vmem((2, NPEER * 8, tile), F32),
            vmem((256, NPEER * GR), BF16),
            vmem((3, 256, 256), BF16),
            vmem((NPEER * GR, 256), BF16),
            vmem((NPEER * GR, tile), BF16),
            vmem((NPEER * GR, tile), BF16),
            vmem((strips, 4, NT * GR, tile), F32),
            vmem((strips, 4, SHARED, tile), F32),
            vmem((strips, 2, 2 * FT * GR, tile), BF16),
            vmem((strips, 2, 2 * FT * GR, tile), BF16),
            vmem((strips, 3, NT * GR, tile), BF16),
            vmem((strips, 2, FT, GR, tile), BF16),
            dma((strips,)),
            dma((strips,)),
            dma((strips, 3)),
            dma((2,)),
            dma((2,)),
            dma((4,)),
            dma((strips,)),
            dma((strips,)),
            dma((strips, 2)),
            dma((strips, 2)),
            dma((strips, 2)),
            dma((strips, 2)),
            dma((strips,)),
            dma((strips,)),
            dma((strips,)),
            dma((strips,)),
            dma((strips,)),
            dma((strips,)),
            dma((strips,)),
            dma((strips, 3)),
        ],
        compiler_params=pltpu.CompilerParams(
            collective_id=0, has_side_effects=True, vmem_limit_bytes=MAIN_VMEM
        ),
    )(in_vmem(send), in_vmem(meta))
    joint, residual = pl.pallas_call(
        place_kernel,
        out_shape=(pltpu.HBM(image, BF16), pltpu.HBM(footprint, BF16)),
        in_specs=[scalars, anywhere, anywhere],
        out_specs=(anywhere, anywhere),
        scratch_shapes=[dma((NPEER + 1,))],
        compiler_params=pltpu.CompilerParams(vmem_limit_bytes=SMALL_VMEM),
    )(offsets, in_vmem(joint), in_vmem(back))
    return joint, residual.reshape(1, foot, foot)


def solution(mesh):
    in_specs = (P(("row", "col"), None, None), P(("row", "col"), None), P(("row", "col"), None))
    out_specs = (P("row", "col", None, None), P(("row", "col"), None, None))
    return jax.shard_map(
        local, mesh=mesh, in_specs=in_specs, out_specs=out_specs, check_vma=False
    )
```

```python
import functools
import math

import jax
import jax.numpy as jnp
import numpy as np
from jax import lax
from jax.experimental import pallas as pl
from jax.experimental.pallas import tpu as pltpu
from jax.sharding import PartitionSpec as P

MESH = pl.DeviceIdType.MESH
FT = 4
NPEER = 32
RES = 16
ROWS7 = 7
NT = 2 * ROWS7
GR = 16
SHARED = 3 * 2 * GR
FLOOR = 0.1
AHEAD = 5
MAIN_VMEM = 44 * 1024 * 1024
SMALL_VMEM = 16 * 1024 * 1024
LAG = (0, 2, 3, 5, 6)
HIGHEST = lax.Precision.HIGHEST
F32 = jnp.float32
BF16 = jnp.bfloat16


def zernike_table():
    table = np.zeros((36, 8, 8))
    term = 0
    for degree in range(8):
        for azimuth in range(-degree, degree + 1, 2):
            order = abs(azimuth)
            angular = np.zeros((8, 8))
            for power in range(order + 1):
                weight = math.comb(order, power)
                if azimuth >= 0 and power % 2 == 0:
                    angular[order - power, power] += weight * (-1) ** (power // 2)
                if azimuth < 0 and power % 2 == 1:
                    angular[order - power, power] += weight * (-1) ** ((power - 1) // 2)
            for step in range((degree - order) // 2 + 1):
                radial = (
                    (-1) ** step
                    * math.factorial(degree - step)
                    / (
                        math.factorial(step)
                        * math.factorial((degree + order) // 2 - step)
                        * math.factorial((degree - order) // 2 - step)
                    )
                )
                square = (degree - 2 * step - order) // 2
                for part in range(square + 1):
                    su, sv = 2 * part, 2 * (square - part)
                    table[term, su:, sv:] += (
                        radial * math.comb(square, part) * angular[: 8 - su, : 8 - sv]
                    )
            term += 1
    return table


def to_local_table(tile):
    foot = FT * tile
    table = zernike_table()
    unit = math.sqrt(2.0) / foot
    sigma = unit * tile / 2
    shift = np.zeros((FT, 8, 8))
    for a in range(FT):
        centre = (a * tile + tile / 2 - foot / 2) * unit
        for i in range(8):
            for m in range(i + 1):
                shift[a, i, m] = math.comb(i, m) * centre ** (i - m) * sigma**m
    local = np.einsum("kij,bim,ajn->kabnm", table, shift, shift)
    to_local = np.zeros((36, RES, 128))
    to_local[:, :, :64] = local.reshape(36, RES, 64)
    return to_local.reshape(36, RES * 128).astype(np.float32)


def iota(shape, dim):
    return lax.broadcasted_iota(jnp.int32, shape, dim)


def to_power(base, exponent):
    square = base * base
    low = jnp.where(lax.rem(exponent, 2) == 1, base, 1.0)
    middle = jnp.where(lax.rem(lax.div(exponent, 2), 2) == 1, square, 1.0)
    return low * middle * jnp.where(lax.div(exponent, 4) == 1, square * square, 1.0)


def kernel(
    send,
    meta_send,
    joint_hbm,
    back,
    recv,
    beams,
    beams_all,
    ret_send,
    meta_all,
    meta_role,
    bbuf,
    xbuf,
    wbuf,
    k_all,
    k_role,
    kt,
    high,
    low,
    sums,
    from_below,
    partial,
    partial_in,
    img,
    jbuf,
    fwd_s,
    fwd_r,
    fwd_l,
    meta_s,
    meta_r,
    meta_l,
    up_s,
    up_r,
    part_s,
    part_r,
    img_s,
    img_r,
    down_s,
    down_r,
    j_s,
    j_r,
    j_l,
    ret_s,
    ret_r,
    ret_l,
):
    row = lax.axis_index("row")
    col = lax.axis_index("col")
    n_row = lax.axis_size("row")
    strips = recv.shape[0]
    tile = recv.shape[-1]
    half = tile // 2
    nx, nz = NPEER // 8, 8
    px, pz = lax.div(col, nz), lax.rem(col, nz)
    side = lax.div(col, RES)
    up = lax.rem(row + 1, n_row)
    below = lax.rem(row + n_row - 1, n_row)
    partner = lax.rem(col + RES, NPEER)

    def at(x, dz):
        return x * nz + lax.rem(pz + dz + nz, nz)

    def peer(i):
        j = lax.div(i, nx)
        last = lax.div(j, nz - 1)
        near = lax.div(j, 2) + 1
        dz = (near + lax.rem(j, 2) * (nz - 2 * near)) * (1 - last)
        return at(lax.rem(px + gray(i + last), nx), dz)

    def gray(i):
        e = lax.rem(i, nx)
        return e + lax.div(e, 2) * (1 - 2 * lax.rem(e, 2))

    barrier = pltpu.get_barrier_semaphore()

    def greet(i, carry):
        pl.semaphore_signal(barrier, inc=1, device_id=(row, peer(i)), device_id_type=MESH)
        return carry

    lax.fori_loop(0, NPEER - 1, greet, 0)
    pl.semaphore_signal(barrier, inc=1, device_id=(up, col), device_id_type=MESH)
    pl.semaphore_signal(barrier, inc=1, device_id=(below, col), device_id_type=MESH)

    def remote(src, dst, send_sem, recv_sem, to_row, to_col):
        return pltpu.make_async_remote_copy(
            src_ref=src,
            dst_ref=dst,
            send_sem=send_sem,
            recv_sem=recv_sem,
            device_id=(to_row, to_col),
            device_id_type=MESH,
        )

    def roles(dx):
        odd = lax.rem(dx, 2)
        pair = lax.div(px, 2)
        return (
            (2, 1, 4 + px),
            (-2, -1, 24 + px),
            (3, 2, 8 + px),
            (-3, -2, 28 + px),
            (4, 3 + 2 * odd, 12 + 6 * odd + pair),
            (1, 0, px),
            (-1, 0, 20 + px),
            (0, 0, 14 + px),
        )

    def send_roles(source, target, send_sem, recv_sem, local_sem):
        def one(i, carry):
            dx = gray(i)
            x = lax.rem(px + dx, nx)
            for dz, away, slot in roles(dx):
                to, centre = at(x, away), at(x, dz)
                if isinstance(away, int) and away == 0:

                    @pl.when(dx != 0)
                    def _(centre=centre, slot=slot, to=to):
                        remote(source(centre), target(slot), send_sem, recv_sem, row, to).start()
                else:
                    remote(source(centre), target(slot), send_sem, recv_sem, row, to).start()
            return carry

        lax.fori_loop(0, nx, one, 0)
        for copy in own_copies(source, target, local_sem):
            copy.start()

    def own_copies(source, target, local_sem):
        return [
            pltpu.make_async_copy(source(at(px, dz)), target(slot), local_sem.at[n])
            for n, (dz, slot) in enumerate(((1, px), (0, 14 + px), (-1, 20 + px)))
        ]

    def strip_ends(s):
        return (lambda j: send.at[j, s]), (lambda slot: recv.at[s, slot])

    def forward(s):
        send_roles(*strip_ends(s), fwd_s.at[s], fwd_r.at[s], fwd_l.at[s])

    meta_ends = (lambda j: meta_send.at[lax.rem(j, RES)]), (lambda slot: meta_role.at[slot])

    def own_meta():
        return pltpu.make_async_copy(
            meta_send.at[lax.rem(col, RES)], meta_all.at[col], meta_l.at[3]
        )

    def send_meta(i, carry):
        to = peer(i)
        remote(
            meta_send.at[lax.rem(to, RES)], meta_all.at[col], meta_s.at[1], meta_r.at[1], row, to
        ).start()
        return carry

    pl.semaphore_wait(barrier, NPEER + 1)
    send_roles(*meta_ends, meta_s.at[0], meta_r.at[0], meta_l)
    lax.fori_loop(0, NPEER - 1, send_meta, 0)
    own_meta().start()
    ahead = min(AHEAD, strips)

    def forward_strip(s, carry):
        forward(s)
        return carry

    lax.fori_loop(0, ahead, forward_strip, 0)

    shape = (128, tile)
    spot = (iota(shape, 1).astype(F32) + (0.5 - tile / 2)) * (2.0 / tile)
    across = jnp.where(iota(shape, 0) < 64, to_power(spot, lax.rem(iota(shape, 0), 8)), 0.0)
    shape = (half, 48)
    spot = ((iota(shape, 0) + side * half).astype(F32) + (0.5 - tile / 2)) * (2.0 / tile)
    whole = to_power(spot, lax.rem(iota(shape, 1), 8))
    first = whole.astype(BF16).astype(F32)
    second = (whole - first).astype(BF16).astype(F32)
    third = whole - first - second
    part = lax.div(iota(shape, 1), 8)
    down = jnp.where(
        part == 5, third, jnp.where(jnp.logical_or(part == 2, part == 4), second, first)
    ).astype(BF16)
    shape = (256, 128)
    spread = jnp.where(iota(shape, 1) == 64 + lax.div(iota(shape, 0), GR), 1.0, 0.0).astype(BF16)

    remotes = NPEER - 3
    arrived = meta_role.at[pl.ds(0, remotes)]
    pltpu.make_async_copy(arrived, arrived, meta_r.at[0]).wait()
    for copy in own_copies(*meta_ends, meta_l):
        copy.wait()
    arrived = meta_all.at[pl.ds(0, NPEER - 1)]
    pltpu.make_async_copy(arrived, arrived, meta_r.at[1]).wait()
    own_meta().wait()
    lane = iota((1, 128), 1)
    own_block = lax.div(iota((8, 128), 1), 8) == iota((8, 128), 0)

    def expand(k, carry):
        for n, meta in enumerate((meta_role, meta_all)):
            values = meta[k]
            bbuf[n, pl.ds(pl.multiple_of(k * 8, 8), 8), :] = jnp.where(
                own_block, jnp.broadcast_to(values, (8, 128)), 0.0
            )
            hot = jnp.where(lane >= 64, values, 0.0)
            xbuf[n, pl.ds(pl.multiple_of(k * GR, GR), GR), :] = jnp.broadcast_to(
                hot, (GR, 128)
            ).astype(BF16)
        return carry

    lax.fori_loop(0, NPEER, expand, 0)
    nt = (((1,), (1,)), ((), ()))

    def same(shape):
        return lax.rem(iota(shape, 0), GR) == lax.rem(iota(shape, 1), GR)

    for n in range(2):
        wbuf[n] = jnp.dot(bbuf[n], across, precision=HIGHEST, preferred_element_type=F32)
        placed = lax.dot_general(spread, xbuf[n], nt, preferred_element_type=F32)
        placed = jnp.where(same(placed.shape), placed, 0.0)
        if n == 0:
            slot = lax.div(iota(placed.shape, 1), GR)
            before = jnp.where(slot < 14, placed, 0.0).astype(BF16)
            after = jnp.where(slot >= 18, placed, 0.0).astype(BF16)
            centre = jnp.where(jnp.logical_and(slot >= 14, slot < 18), placed, 0.0).astype(BF16)
            k_role[0] = before[:, :256]
            k_role[1] = centre[:, 128:384]
            k_role[2] = after[:, 256:]
            picked = lax.dot_general(xbuf[n], spread, nt, preferred_element_type=F32)
            kt[...] = jnp.where(same(picked.shape), picked, 0.0).astype(BF16)
        else:
            k_all[...] = placed.astype(BF16)

    def beam(k, carry):
        for n, target in enumerate((beams, beams_all)):
            wide = wbuf[n, pl.ds(pl.multiple_of(k * 8, 8), 8), :]
            one = wide.astype(BF16).astype(F32)
            rest = wide - one
            two = rest.astype(BF16).astype(F32)
            three = rest - two
            terms = jnp.concatenate([one, two, one, three, two, one], axis=0).astype(BF16)
            field = jnp.dot(down, terms, preferred_element_type=F32)
            power = (field * field).astype(BF16)
            target[:, k] = power.reshape(strips, GR, tile)
        return carry

    lax.fori_loop(0, NPEER, beam, 0)

    def split(product):
        step = 8
        for c in range(NPEER // step):
            values = product(c * step, (c + 1) * step).reshape(step * GR, tile)
            some = slice(c * step * GR, (c + 1) * step * GR)
            rounded = values.astype(BF16)
            high[some, :] = rounded
            low[some, :] = (values - rounded.astype(F32)).astype(BF16)

    def add_up(matrix, start, size):
        some = slice(start, start + size)
        return jnp.dot(matrix, high[some, :], preferred_element_type=F32) + jnp.dot(
            matrix, low[some, :], preferred_element_type=F32
        )

    last = NT * GR - SHARED
    own = 2 * FT * GR

    def up_copy(s):
        return remote(
            sums.at[s, :, pl.ds(last, SHARED), :],
            from_below.at[s],
            up_s.at[s],
            up_r.at[s],
            up,
            col,
        )

    def partial_copies(s):
        return [
            remote(
                partial.at[s, n],
                partial_in.at[s, n],
                part_s.at[s, n],
                part_r.at[s, n],
                row,
                at(px, away),
            )
            for n, away in enumerate((1, -1))
        ]

    def image_copies(s):
        return [
            remote(
                img.at[s, 1, pl.ds(0, own), :],
                img.at[s, 2 * n, pl.ds(0, own), :],
                img_s.at[s, n],
                img_r.at[s, n],
                row,
                at(px, away),
            )
            for n, away in enumerate((-1, 1))
        ]

    def down_copy(s):
        return remote(
            img.at[s, :, pl.ds(0, SHARED), :],
            img.at[s, :, pl.ds(last, SHARED), :],
            down_s.at[s],
            down_r.at[s],
            below,
            col,
        )

    def joint_copies(s):
        rows = pl.ds(pl.multiple_of(side * half + s * GR, GR), GR)
        return (
            pltpu.make_async_copy(jbuf.at[s, side], joint_hbm.at[:, 0, rows, :], j_l.at[s]),
            remote(
                jbuf.at[s, 1 - side],
                joint_hbm.at[:, 0, rows, :],
                j_s.at[s],
                j_r.at[s],
                row,
                partner,
            ),
        )

    def sum_strip(s):
        strip = recv.at[s, pl.ds(0, remotes)]
        pltpu.make_async_copy(strip, strip, fwd_r.at[s]).wait()
        for copy in own_copies(*strip_ends(s), fwd_l.at[s]):
            copy.wait()
        split(lambda a, b: recv[s, a:b].astype(F32) * beams[s, a:b].astype(F32))
        for n in range(3):
            sums[s, n] = add_up(k_role[n, : NT * GR, :], n * 128, 256)

        def squares(a, b):
            power = beams_all[s, a:b].astype(F32)
            return power * power

        split(squares)
        sums[s, 3] = add_up(k_all[: NT * GR, :], 0, NPEER * GR)
        up_copy(s).start()

    def partial_strip(s):
        up_copy(s).wait_recv()
        for n in range(2):
            partial[s, n, :SHARED, :] = (
                sums[s, 2 * n, :SHARED, :] + from_below[s, 2 * n]
            ).astype(BF16)
            partial[s, n, SHARED:, :] = sums[s, 2 * n, SHARED:own, :].astype(BF16)
        for copy in partial_copies(s):
            copy.start()

    def image_strip(s):
        for copy in partial_copies(s):
            copy.wait_recv()
        off = partial_in[s, 0].astype(F32) + partial_in[s, 1].astype(F32)
        numer = sums[s, 1, :SHARED, :] + from_below[s, 1] + off[:SHARED]
        weigh = jnp.maximum(sums[s, 3, :SHARED, :] + from_below[s, 3], FLOOR)
        img[s, 1, :SHARED, :] = (numer / weigh).astype(BF16)
        numer = sums[s, 1, SHARED:own, :] + off[SHARED:]
        weigh = jnp.maximum(sums[s, 3, SHARED:own, :], FLOOR)
        img[s, 1, SHARED:own, :] = (numer / weigh).astype(BF16)
        for copy in image_copies(s):
            copy.start()
        for r in range(FT):
            for h in range(2):
                first = (r * 2 + h) * GR
                jbuf[s, h, r] = img[s, 1, first : first + GR, :]
        for copy in joint_copies(s):
            copy.start()

    def pass_strip(s):
        for copy in image_copies(s):
            copy.wait_recv()
        down_copy(s).start()

    def own_back(s):
        return [
            pltpu.make_async_copy(
                ret_send.at[s, slot], back.at[at(px, dz), s], ret_l.at[s, n]
            )
            for n, (dz, slot) in enumerate(((1, px), (0, 14 + px), (-1, 20 + px)))
        ]

    def residual_strip(s):
        down_copy(s).wait_recv()
        for n, a, b in ((0, 0, 7), (0, 7, 14), (1, 14, 18), (2, 18, 25), (2, 25, 32)):
            mine = jnp.dot(
                kt[a * GR : b * GR, : NT * GR], img[s, n], preferred_element_type=F32
            ).reshape(b - a, GR, tile)
            left = recv[s, a:b].astype(F32) - beams[s, a:b].astype(F32) * mine
            ret_send[s, a:b] = left.astype(BF16)

        def one(i, carry):
            dx = gray(i)
            x = lax.rem(px + dx, nx)
            odd = lax.rem(dx, 2)
            ways = (
                (1, -1, 4 + x),
                (-1, 1, 24 + x),
                (1, -2, 8 + x),
                (-1, 2, 28 + x),
                (1 - 2 * odd, 5 - 2 * odd, 12 + 6 * odd + lax.div(x, 2)),
                (1, 0, x),
                (-1, 0, 20 + x),
                (0, 0, 14 + x),
            )
            for dz, away, slot in ways:

                def go(dz=dz, away=away, slot=slot):
                    remote(
                        ret_send.at[s, slot],
                        back.at[at(px, dz), s],
                        ret_s.at[s],
                        ret_r.at[s],
                        row,
                        at(x, away),
                    ).start()

                if isinstance(away, int) and away == 0:
                    pl.when(dx != 0)(go)
                else:
                    go()
            return carry

        lax.fori_loop(0, nx, one, 0)
        for copy in own_back(s):
            copy.start()

    stages = (sum_strip, partial_strip, image_strip, pass_strip, residual_strip)

    def step(i, carry):
        for n in (0, 1, 2, 3, 4):
            pl.when(jnp.logical_and(i >= LAG[n], i < strips + LAG[n]))(lambda n=n: stages[n](i - LAG[n]))
        pl.when(i + ahead < strips)(lambda: forward(i + ahead))
        return carry

    lax.fori_loop(0, strips + LAG[-1], step, 0)

    sent = meta_role.at[pl.ds(0, remotes)]
    pltpu.make_async_copy(sent, sent, meta_s.at[0]).wait()
    sent = meta_all.at[pl.ds(0, NPEER - 1)]
    pltpu.make_async_copy(sent, sent, meta_s.at[1]).wait()

    def drain(s, carry):
        sent = recv.at[s, pl.ds(0, remotes)]
        pltpu.make_async_copy(sent, sent, fwd_s.at[s]).wait()
        up_copy(s).wait_send()
        for copy in partial_copies(s):
            copy.wait_send()
        for copy in image_copies(s):
            copy.wait_send()
        down_copy(s).wait_send()
        for copy in joint_copies(s):
            copy.wait()
        sent = ret_send.at[s, pl.ds(0, remotes)]
        pltpu.make_async_copy(sent, sent, ret_s.at[s]).wait()
        pltpu.make_async_copy(sent, sent, ret_r.at[s]).wait()
        for copy in own_back(s):
            copy.wait()
        return carry

    lax.fori_loop(0, strips, drain, 0)


def gather_kernel(off_ref, coef_ref, table, d_hbm, send, meta, to_local, sem, table_sem):
    strips, tile = send.shape[1], send.shape[3]
    row = lax.axis_index("row")
    top = off_ref[0, 0]
    start = lax.rem(off_ref[0, 1] + FT * top, NPEER)

    def move(q, h):
        t = lax.rem(q - start + NPEER, RES)
        first = (lax.div(t, FT) * 2 + h) * strips
        across = pl.multiple_of(lax.rem(t, FT) * tile, tile)
        to = h * RES + q
        return pltpu.make_async_copy(
            d_hbm.at[pl.ds(first, strips), :, pl.ds(across, tile)], send.at[to], sem.at[to]
        )

    moves = [move(q, h) for q in range(RES) for h in range(2)]
    load = pltpu.make_async_copy(table, to_local, table_sem)
    load.start()
    for copy in moves:
        copy.start()
    load.wait()
    flat = jnp.dot(
        coef_ref[...].astype(F32), to_local[...], precision=HIGHEST, preferred_element_type=F32
    )
    lane = iota((1, 128), 1)
    for t in range(RES):
        place = lax.rem(start + t, NPEER)
        target = (top - FT * row + t // FT) * 2 + lax.div(place, RES)
        meta[lax.rem(place, RES)] = jnp.where(
            lane == 64 + target, 1.0, flat[:, t * 128 : (t + 1) * 128]
        )
    for copy in moves:
        copy.wait()


def place_kernel(off_ref, joint, back, joint_out, out_hbm, sem):
    strips, tile = back.shape[1], back.shape[3]
    start = lax.rem(off_ref[0, 1] + FT * off_ref[0, 0], NPEER)

    def move(t, h):
        q = lax.rem(start + t, RES)
        rows = pl.ds(((t // FT) * 2 + h) * strips, strips)
        across = pl.ds((t % FT) * tile, tile)
        return pltpu.make_async_copy(
            back.at[h * RES + q], out_hbm.at[rows, :, across], sem.at[t * 2 + h]
        )

    moves = [move(t, h) for t in range(RES) for h in range(2)]
    moves.append(pltpu.make_async_copy(joint, joint_out, sem.at[NPEER]))
    for copy in moves:
        copy.start()
    for copy in moves:
        copy.wait()


def local(dirty, coefs, offsets):
    foot = dirty.shape[1]
    tile = foot // FT
    half = tile // 2
    strips = half // GR
    vmem = pltpu.VMEM
    dma = pltpu.SemaphoreType.DMA
    tiles = (strips, NPEER, GR, tile)
    by_peer = (NPEER, strips, GR, tile)
    footprint = (foot // GR, GR, foot)
    image = (FT, 1, tile, tile)
    anywhere = pl.BlockSpec(memory_space=pl.ANY)
    whole = pl.BlockSpec(memory_space=pltpu.VMEM)
    scalars = pl.BlockSpec(memory_space=pltpu.SMEM)
    in_hbm = functools.partial(pltpu.with_memory_space_constraint, memory_space=pltpu.HBM)
    in_vmem = functools.partial(pltpu.with_memory_space_constraint, memory_space=pltpu.VMEM)
    offsets = in_hbm(offsets)
    send, meta = pl.pallas_call(
        gather_kernel,
        out_shape=(pltpu.VMEM(by_peer, BF16), pltpu.VMEM((RES, 1, 128), F32)),
        in_specs=[scalars, whole, anywhere, anywhere],
        out_specs=(anywhere, whole),
        scratch_shapes=[vmem((36, RES * 128), F32), dma((NPEER,)), dma],
        compiler_params=pltpu.CompilerParams(vmem_limit_bytes=SMALL_VMEM),
    )(
        offsets,
        in_hbm(coefs),
        in_hbm(jnp.asarray(to_local_table(tile))),
        in_hbm(dirty.reshape(footprint)),
    )
    joint, back = pl.pallas_call(
        kernel,
        out_shape=(pltpu.VMEM(image, BF16), pltpu.VMEM(by_peer, BF16)),
        in_specs=[anywhere, anywhere],
        out_specs=(anywhere, anywhere),
        scratch_shapes=[
            vmem(tiles, BF16),
            vmem(tiles, BF16),
            vmem(tiles, BF16),
            vmem(tiles, BF16),
            vmem((NPEER, 1, 128), F32),
            vmem((NPEER, 1, 128), F32),
            vmem((2, NPEER * 8, 128), F32),
            vmem((2, NPEER * GR, 128), BF16),
            vmem((2, NPEER * 8, tile), F32),
            vmem((256, NPEER * GR), BF16),
            vmem((3, 256, 256), BF16),
            vmem((NPEER * GR, 256), BF16),
            vmem((NPEER * GR, tile), BF16),
            vmem((NPEER * GR, tile), BF16),
            vmem((strips, 4, NT * GR, tile), F32),
            vmem((strips, 4, SHARED, tile), F32),
            vmem((strips, 2, 2 * FT * GR, tile), BF16),
            vmem((strips, 2, 2 * FT * GR, tile), BF16),
            vmem((strips, 3, NT * GR, tile), BF16),
            vmem((strips, 2, FT, GR, tile), BF16),
            dma((strips,)),
            dma((strips,)),
            dma((strips, 3)),
            dma((2,)),
            dma((2,)),
            dma((4,)),
            dma((strips,)),
            dma((strips,)),
            dma((strips, 2)),
            dma((strips, 2)),
            dma((strips, 2)),
            dma((strips, 2)),
            dma((strips,)),
            dma((strips,)),
            dma((strips,)),
            dma((strips,)),
            dma((strips,)),
            dma((strips,)),
            dma((strips,)),
            dma((strips, 3)),
        ],
        compiler_params=pltpu.CompilerParams(
            collective_id=0, has_side_effects=True, vmem_limit_bytes=MAIN_VMEM
        ),
    )(in_vmem(send), in_vmem(meta))
    joint, residual = pl.pallas_call(
        place_kernel,
        out_shape=(pltpu.HBM(image, BF16), pltpu.HBM(footprint, BF16)),
        in_specs=[scalars, anywhere, anywhere],
        out_specs=(anywhere, anywhere),
        scratch_shapes=[dma((NPEER + 1,))],
        compiler_params=pltpu.CompilerParams(vmem_limit_bytes=SMALL_VMEM),
    )(offsets, in_vmem(joint), in_vmem(back))
    return joint, residual.reshape(1, foot, foot)


def solution(mesh):
    in_specs = (P(("row", "col"), None, None), P(("row", "col"), None), P(("row", "col"), None))
    out_specs = (P("row", "col", None, None), P(("row", "col"), None, None))
    return jax.shard_map(
        local, mesh=mesh, in_specs=in_specs, out_specs=out_specs, check_vma=False
    )
```

```python
import functools
import math

import jax
import jax.numpy as jnp
import numpy as np
from jax import lax
from jax.experimental import pallas as pl
from jax.experimental.pallas import tpu as pltpu
from jax.sharding import PartitionSpec as P

MESH = pl.DeviceIdType.MESH
FT = 4
NPEER = 32
RES = 16
ROWS7 = 7
NT = 2 * ROWS7
GR = 16
SHARED = 3 * 2 * GR
FLOOR = 0.1
AHEAD = 4
MAIN_VMEM = 44 * 1024 * 1024
SMALL_VMEM = 16 * 1024 * 1024
LAG = (0, 2, 3, 5, 6)
HIGHEST = lax.Precision.HIGHEST
F32 = jnp.float32
BF16 = jnp.bfloat16


def zernike_table():
    table = np.zeros((36, 8, 8))
    term = 0
    for degree in range(8):
        for azimuth in range(-degree, degree + 1, 2):
            order = abs(azimuth)
            angular = np.zeros((8, 8))
            for power in range(order + 1):
                weight = math.comb(order, power)
                if azimuth >= 0 and power % 2 == 0:
                    angular[order - power, power] += weight * (-1) ** (power // 2)
                if azimuth < 0 and power % 2 == 1:
                    angular[order - power, power] += weight * (-1) ** ((power - 1) // 2)
            for step in range((degree - order) // 2 + 1):
                radial = (
                    (-1) ** step
                    * math.factorial(degree - step)
                    / (
                        math.factorial(step)
                        * math.factorial((degree + order) // 2 - step)
                        * math.factorial((degree - order) // 2 - step)
                    )
                )
                square = (degree - 2 * step - order) // 2
                for part in range(square + 1):
                    su, sv = 2 * part, 2 * (square - part)
                    table[term, su:, sv:] += (
                        radial * math.comb(square, part) * angular[: 8 - su, : 8 - sv]
                    )
            term += 1
    return table


def to_local_table(tile):
    foot = FT * tile
    table = zernike_table()
    unit = math.sqrt(2.0) / foot
    sigma = unit * tile / 2
    shift = np.zeros((FT, 8, 8))
    for a in range(FT):
        centre = (a * tile + tile / 2 - foot / 2) * unit
        for i in range(8):
            for m in range(i + 1):
                shift[a, i, m] = math.comb(i, m) * centre ** (i - m) * sigma**m
    local = np.einsum("kij,bim,ajn->kabnm", table, shift, shift)
    to_local = np.zeros((36, RES, 128))
    to_local[:, :, :64] = local.reshape(36, RES, 64)
    return to_local.reshape(36, RES * 128).astype(np.float32)


def iota(shape, dim):
    return lax.broadcasted_iota(jnp.int32, shape, dim)


def to_power(base, exponent):
    square = base * base
    low = jnp.where(lax.rem(exponent, 2) == 1, base, 1.0)
    middle = jnp.where(lax.rem(lax.div(exponent, 2), 2) == 1, square, 1.0)
    return low * middle * jnp.where(lax.div(exponent, 4) == 1, square * square, 1.0)


def kernel(
    send,
    meta_send,
    joint_hbm,
    back,
    recv,
    beams,
    beams_all,
    ret_send,
    meta_all,
    meta_role,
    bbuf,
    xbuf,
    wbuf,
    k_all,
    k_role,
    kt,
    high,
    low,
    sums,
    from_below,
    partial,
    partial_in,
    img,
    jbuf,
    fwd_s,
    fwd_r,
    fwd_l,
    meta_s,
    meta_r,
    meta_l,
    up_s,
    up_r,
    part_s,
    part_r,
    img_s,
    img_r,
    down_s,
    down_r,
    j_s,
    j_r,
    j_l,
    ret_s,
    ret_r,
    ret_l,
):
    row = lax.axis_index("row")
    col = lax.axis_index("col")
    n_row = lax.axis_size("row")
    strips = recv.shape[0]
    tile = recv.shape[-1]
    half = tile // 2
    nx, nz = NPEER // 8, 8
    px, pz = lax.div(col, nz), lax.rem(col, nz)
    side = lax.div(col, RES)
    up = lax.rem(row + 1, n_row)
    below = lax.rem(row + n_row - 1, n_row)
    partner = lax.rem(col + RES, NPEER)

    def at(x, dz):
        return x * nz + lax.rem(pz + dz + nz, nz)

    def peer(i):
        j = lax.div(i, nx)
        last = lax.div(j, nz - 1)
        near = lax.div(j, 2) + 1
        dz = (near + lax.rem(j, 2) * (nz - 2 * near)) * (1 - last)
        return at(lax.rem(px + gray(i + last), nx), dz)

    def gray(i):
        e = lax.rem(i, nx)
        return e + lax.div(e, 2) * (1 - 2 * lax.rem(e, 2))

    barrier = pltpu.get_barrier_semaphore()

    def greet(i, carry):
        pl.semaphore_signal(barrier, inc=1, device_id=(row, peer(i)), device_id_type=MESH)
        return carry

    lax.fori_loop(0, NPEER - 1, greet, 0)
    pl.semaphore_signal(barrier, inc=1, device_id=(up, col), device_id_type=MESH)
    pl.semaphore_signal(barrier, inc=1, device_id=(below, col), device_id_type=MESH)

    def remote(src, dst, send_sem, recv_sem, to_row, to_col):
        return pltpu.make_async_remote_copy(
            src_ref=src,
            dst_ref=dst,
            send_sem=send_sem,
            recv_sem=recv_sem,
            device_id=(to_row, to_col),
            device_id_type=MESH,
        )

    def roles(dx):
        odd = lax.rem(dx, 2)
        pair = lax.div(px, 2)
        return (
            (2, 1, 4 + px),
            (-2, -1, 24 + px),
            (3, 2, 8 + px),
            (-3, -2, 28 + px),
            (4, 3 + 2 * odd, 12 + 6 * odd + pair),
            (1, 0, px),
            (-1, 0, 20 + px),
            (0, 0, 14 + px),
        )

    def send_roles(source, target, send_sem, recv_sem, local_sem):
        def one(i, carry):
            dx = gray(i)
            x = lax.rem(px + dx, nx)
            for dz, away, slot in roles(dx):
                to, centre = at(x, away), at(x, dz)
                if isinstance(away, int) and away == 0:

                    @pl.when(dx != 0)
                    def _(centre=centre, slot=slot, to=to):
                        remote(source(centre), target(slot), send_sem, recv_sem, row, to).start()
                else:
                    remote(source(centre), target(slot), send_sem, recv_sem, row, to).start()
            return carry

        lax.fori_loop(0, nx, one, 0)
        for copy in own_copies(source, target, local_sem):
            copy.start()

    def own_copies(source, target, local_sem):
        return [
            pltpu.make_async_copy(source(at(px, dz)), target(slot), local_sem.at[n])
            for n, (dz, slot) in enumerate(((1, px), (0, 14 + px), (-1, 20 + px)))
        ]

    def strip_ends(s):
        return (lambda j: send.at[j, s]), (lambda slot: recv.at[s, slot])

    def forward(s):
        send_roles(*strip_ends(s), fwd_s.at[s], fwd_r.at[s], fwd_l.at[s])

    meta_ends = (lambda j: meta_send.at[lax.rem(j, RES)]), (lambda slot: meta_role.at[slot])

    def own_meta():
        return pltpu.make_async_copy(
            meta_send.at[lax.rem(col, RES)], meta_all.at[col], meta_l.at[3]
        )

    def send_meta(i, carry):
        to = peer(i)
        remote(
            meta_send.at[lax.rem(to, RES)], meta_all.at[col], meta_s.at[1], meta_r.at[1], row, to
        ).start()
        return carry

    pl.semaphore_wait(barrier, NPEER + 1)
    send_roles(*meta_ends, meta_s.at[0], meta_r.at[0], meta_l)
    lax.fori_loop(0, NPEER - 1, send_meta, 0)
    own_meta().start()
    ahead = min(AHEAD, strips)

    def forward_strip(s, carry):
        forward(s)
        return carry

    lax.fori_loop(0, ahead, forward_strip, 0)

    shape = (128, tile)
    spot = (iota(shape, 1).astype(F32) + (0.5 - tile / 2)) * (2.0 / tile)
    across = jnp.where(iota(shape, 0) < 64, to_power(spot, lax.rem(iota(shape, 0), 8)), 0.0)
    shape = (half, 48)
    spot = ((iota(shape, 0) + side * half).astype(F32) + (0.5 - tile / 2)) * (2.0 / tile)
    whole = to_power(spot, lax.rem(iota(shape, 1), 8))
    first = whole.astype(BF16).astype(F32)
    second = (whole - first).astype(BF16).astype(F32)
    third = whole - first - second
    part = lax.div(iota(shape, 1), 8)
    down = jnp.where(
        part == 5, third, jnp.where(jnp.logical_or(part == 2, part == 4), second, first)
    ).astype(BF16)
    shape = (256, 128)
    spread = jnp.where(iota(shape, 1) == 64 + lax.div(iota(shape, 0), GR), 1.0, 0.0).astype(BF16)

    remotes = NPEER - 3
    arrived = meta_role.at[pl.ds(0, remotes)]
    pltpu.make_async_copy(arrived, arrived, meta_r.at[0]).wait()
    for copy in own_copies(*meta_ends, meta_l):
        copy.wait()
    arrived = meta_all.at[pl.ds(0, NPEER - 1)]
    pltpu.make_async_copy(arrived, arrived, meta_r.at[1]).wait()
    own_meta().wait()
    lane = iota((1, 128), 1)
    own_block = lax.div(iota((8, 128), 1), 8) == iota((8, 128), 0)

    def expand(k, carry):
        for n, meta in enumerate((meta_role, meta_all)):
            values = meta[k]
            bbuf[n, pl.ds(pl.multiple_of(k * 8, 8), 8), :] = jnp.where(
                own_block, jnp.broadcast_to(values, (8, 128)), 0.0
            )
            hot = jnp.where(lane >= 64, values, 0.0)
            xbuf[n, pl.ds(pl.multiple_of(k * GR, GR), GR), :] = jnp.broadcast_to(
                hot, (GR, 128)
            ).astype(BF16)
        return carry

    lax.fori_loop(0, NPEER, expand, 0)
    nt = (((1,), (1,)), ((), ()))

    def same(shape):
        return lax.rem(iota(shape, 0), GR) == lax.rem(iota(shape, 1), GR)

    for n in range(2):
        wbuf[n] = jnp.dot(bbuf[n], across, precision=HIGHEST, preferred_element_type=F32)
        placed = lax.dot_general(spread, xbuf[n], nt, preferred_element_type=F32)
        placed = jnp.where(same(placed.shape), placed, 0.0)
        if n == 0:
            slot = lax.div(iota(placed.shape, 1), GR)
            before = jnp.where(slot < 14, placed, 0.0).astype(BF16)
            after = jnp.where(slot >= 18, placed, 0.0).astype(BF16)
            centre = jnp.where(jnp.logical_and(slot >= 14, slot < 18), placed, 0.0).astype(BF16)
            k_role[0] = before[:, :256]
            k_role[1] = centre[:, 128:384]
            k_role[2] = after[:, 256:]
            picked = lax.dot_general(xbuf[n], spread, nt, preferred_element_type=F32)
            kt[...] = jnp.where(same(picked.shape), picked, 0.0).astype(BF16)
        else:
            k_all[...] = placed.astype(BF16)

    def beam(k, carry):
        for n, target in enumerate((beams, beams_all)):
            wide = wbuf[n, pl.ds(pl.multiple_of(k * 8, 8), 8), :]
            one = wide.astype(BF16).astype(F32)
            rest = wide - one
            two = rest.astype(BF16).astype(F32)
            three = rest - two
            terms = jnp.concatenate([one, two, one, three, two, one], axis=0).astype(BF16)
            field = jnp.dot(down, terms, preferred_element_type=F32)
            power = (field * field).astype(BF16)
            target[:, k] = power.reshape(strips, GR, tile)
        return carry

    lax.fori_loop(0, NPEER, beam, 0)

    def split(product):
        step = 8
        for c in range(NPEER // step):
            values = product(c * step, (c + 1) * step).reshape(step * GR, tile)
            some = slice(c * step * GR, (c + 1) * step * GR)
            rounded = values.astype(BF16)
            high[some, :] = rounded
            low[some, :] = (values - rounded.astype(F32)).astype(BF16)

    def add_up(matrix, start, size):
        some = slice(start, start + size)
        return jnp.dot(matrix, high[some, :], preferred_element_type=F32) + jnp.dot(
            matrix, low[some, :], preferred_element_type=F32
        )

    last = NT * GR - SHARED
    own = 2 * FT * GR

    def up_copy(s):
        return remote(
            sums.at[s, :, pl.ds(last, SHARED), :],
            from_below.at[s],
            up_s.at[s],
            up_r.at[s],
            up,
            col,
        )

    def partial_copies(s):
        return [
            remote(
                partial.at[s, n],
                partial_in.at[s, n],
                part_s.at[s, n],
                part_r.at[s, n],
                row,
                at(px, away),
            )
            for n, away in enumerate((1, -1))
        ]

    def image_copies(s):
        return [
            remote(
                img.at[s, 1, pl.ds(0, own), :],
                img.at[s, 2 * n, pl.ds(0, own), :],
                img_s.at[s, n],
                img_r.at[s, n],
                row,
                at(px, away),
            )
            for n, away in enumerate((-1, 1))
        ]

    def down_copy(s):
        return remote(
            img.at[s, :, pl.ds(0, SHARED), :],
            img.at[s, :, pl.ds(last, SHARED), :],
            down_s.at[s],
            down_r.at[s],
            below,
            col,
        )

    def joint_copies(s):
        rows = pl.ds(pl.multiple_of(side * half + s * GR, GR), GR)
        return (
            pltpu.make_async_copy(jbuf.at[s, side], joint_hbm.at[:, 0, rows, :], j_l.at[s]),
            remote(
                jbuf.at[s, 1 - side],
                joint_hbm.at[:, 0, rows, :],
                j_s.at[s],
                j_r.at[s],
                row,
                partner,
            ),
        )

    def sum_strip(s):
        strip = recv.at[s, pl.ds(0, remotes)]
        pltpu.make_async_copy(strip, strip, fwd_r.at[s]).wait()
        for copy in own_copies(*strip_ends(s), fwd_l.at[s]):
            copy.wait()
        split(lambda a, b: recv[s, a:b].astype(F32) * beams[s, a:b].astype(F32))
        for n in range(3):
            sums[s, n] = add_up(k_role[n, : NT * GR, :], n * 128, 256)

        def squares(a, b):
            power = beams_all[s, a:b].astype(F32)
            return power * power

        split(squares)
        sums[s, 3] = add_up(k_all[: NT * GR, :], 0, NPEER * GR)
        up_copy(s).start()

    def partial_strip(s):
        up_copy(s).wait_recv()
        for n in range(2):
            partial[s, n, :SHARED, :] = (
                sums[s, 2 * n, :SHARED, :] + from_below[s, 2 * n]
            ).astype(BF16)
            partial[s, n, SHARED:, :] = sums[s, 2 * n, SHARED:own, :].astype(BF16)
        for copy in partial_copies(s):
            copy.start()

    def image_strip(s):
        for copy in partial_copies(s):
            copy.wait_recv()
        off = partial_in[s, 0].astype(F32) + partial_in[s, 1].astype(F32)
        numer = sums[s, 1, :SHARED, :] + from_below[s, 1] + off[:SHARED]
        weigh = jnp.maximum(sums[s, 3, :SHARED, :] + from_below[s, 3], FLOOR)
        img[s, 1, :SHARED, :] = (numer / weigh).astype(BF16)
        numer = sums[s, 1, SHARED:own, :] + off[SHARED:]
        weigh = jnp.maximum(sums[s, 3, SHARED:own, :], FLOOR)
        img[s, 1, SHARED:own, :] = (numer / weigh).astype(BF16)
        for copy in image_copies(s):
            copy.start()
        for r in range(FT):
            for h in range(2):
                first = (r * 2 + h) * GR
                jbuf[s, h, r] = img[s, 1, first : first + GR, :]
        for copy in joint_copies(s):
            copy.start()

    def pass_strip(s):
        for copy in image_copies(s):
            copy.wait_recv()
        down_copy(s).start()

    def own_back(s):
        return [
            pltpu.make_async_copy(
                ret_send.at[s, slot], back.at[at(px, dz), s], ret_l.at[s, n]
            )
            for n, (dz, slot) in enumerate(((1, px), (0, 14 + px), (-1, 20 + px)))
        ]

    def residual_strip(s):
        down_copy(s).wait_recv()
        for n, a, b in ((0, 0, 7), (0, 7, 14), (1, 14, 18), (2, 18, 25), (2, 25, 32)):
            mine = jnp.dot(
                kt[a * GR : b * GR, : NT * GR], img[s, n], preferred_element_type=F32
            ).reshape(b - a, GR, tile)
            left = recv[s, a:b].astype(F32) - beams[s, a:b].astype(F32) * mine
            ret_send[s, a:b] = left.astype(BF16)

        def one(i, carry):
            dx = gray(i)
            x = lax.rem(px + dx, nx)
            odd = lax.rem(dx, 2)
            ways = (
                (1, -1, 4 + x),
                (-1, 1, 24 + x),
                (1, -2, 8 + x),
                (-1, 2, 28 + x),
                (1 - 2 * odd, 5 - 2 * odd, 12 + 6 * odd + lax.div(x, 2)),
                (1, 0, x),
                (-1, 0, 20 + x),
                (0, 0, 14 + x),
            )
            for dz, away, slot in ways:

                def go(dz=dz, away=away, slot=slot):
                    remote(
                        ret_send.at[s, slot],
                        back.at[at(px, dz), s],
                        ret_s.at[s],
                        ret_r.at[s],
                        row,
                        at(x, away),
                    ).start()

                if isinstance(away, int) and away == 0:
                    pl.when(dx != 0)(go)
                else:
                    go()
            return carry

        lax.fori_loop(0, nx, one, 0)
        for copy in own_back(s):
            copy.start()

    stages = (sum_strip, partial_strip, image_strip, pass_strip, residual_strip)

    def step(i, carry):
        for n in (0, 1, 2, 3, 4):
            pl.when(jnp.logical_and(i >= LAG[n], i < strips + LAG[n]))(lambda n=n: stages[n](i - LAG[n]))
        pl.when(i + ahead < strips)(lambda: forward(i + ahead))
        return carry

    lax.fori_loop(0, strips + LAG[-1], step, 0)

    sent = meta_role.at[pl.ds(0, remotes)]
    pltpu.make_async_copy(sent, sent, meta_s.at[0]).wait()
    sent = meta_all.at[pl.ds(0, NPEER - 1)]
    pltpu.make_async_copy(sent, sent, meta_s.at[1]).wait()

    def drain(s, carry):
        sent = recv.at[s, pl.ds(0, remotes)]
        pltpu.make_async_copy(sent, sent, fwd_s.at[s]).wait()
        up_copy(s).wait_send()
        for copy in partial_copies(s):
            copy.wait_send()
        for copy in image_copies(s):
            copy.wait_send()
        down_copy(s).wait_send()
        for copy in joint_copies(s):
            copy.wait()
        sent = ret_send.at[s, pl.ds(0, remotes)]
        pltpu.make_async_copy(sent, sent, ret_s.at[s]).wait()
        pltpu.make_async_copy(sent, sent, ret_r.at[s]).wait()
        for copy in own_back(s):
            copy.wait()
        return carry

    lax.fori_loop(0, strips, drain, 0)


def gather_kernel(off_ref, coef_ref, table, d_hbm, send, meta, to_local, sem, table_sem):
    strips, tile = send.shape[1], send.shape[3]
    row = lax.axis_index("row")
    top = off_ref[0, 0]
    start = lax.rem(off_ref[0, 1] + FT * top, NPEER)

    def move(q, h):
        t = lax.rem(q - start + NPEER, RES)
        first = (lax.div(t, FT) * 2 + h) * strips
        across = pl.multiple_of(lax.rem(t, FT) * tile, tile)
        to = h * RES + q
        return pltpu.make_async_copy(
            d_hbm.at[pl.ds(first, strips), :, pl.ds(across, tile)], send.at[to], sem.at[to]
        )

    moves = [move(q, h) for q in range(RES) for h in range(2)]
    load = pltpu.make_async_copy(table, to_local, table_sem)
    load.start()
    for copy in moves:
        copy.start()
    load.wait()
    flat = jnp.dot(
        coef_ref[...].astype(F32), to_local[...], precision=HIGHEST, preferred_element_type=F32
    )
    lane = iota((1, 128), 1)
    for t in range(RES):
        place = lax.rem(start + t, NPEER)
        target = (top - FT * row + t // FT) * 2 + lax.div(place, RES)
        meta[lax.rem(place, RES)] = jnp.where(
            lane == 64 + target, 1.0, flat[:, t * 128 : (t + 1) * 128]
        )
    for copy in moves:
        copy.wait()


def place_kernel(off_ref, joint, back, joint_out, out_hbm, sem):
    strips, tile = back.shape[1], back.shape[3]
    start = lax.rem(off_ref[0, 1] + FT * off_ref[0, 0], NPEER)

    def move(t, h):
        q = lax.rem(start + t, RES)
        rows = pl.ds(((t // FT) * 2 + h) * strips, strips)
        across = pl.ds((t % FT) * tile, tile)
        return pltpu.make_async_copy(
            back.at[h * RES + q], out_hbm.at[rows, :, across], sem.at[t * 2 + h]
        )

    moves = [move(t, h) for t in range(RES) for h in range(2)]
    moves.append(pltpu.make_async_copy(joint, joint_out, sem.at[NPEER]))
    for copy in moves:
        copy.start()
    for copy in moves:
        copy.wait()


def local(dirty, coefs, offsets):
    foot = dirty.shape[1]
    tile = foot // FT
    half = tile // 2
    strips = half // GR
    vmem = pltpu.VMEM
    dma = pltpu.SemaphoreType.DMA
    tiles = (strips, NPEER, GR, tile)
    by_peer = (NPEER, strips, GR, tile)
    footprint = (foot // GR, GR, foot)
    image = (FT, 1, tile, tile)
    anywhere = pl.BlockSpec(memory_space=pl.ANY)
    whole = pl.BlockSpec(memory_space=pltpu.VMEM)
    scalars = pl.BlockSpec(memory_space=pltpu.SMEM)
    in_hbm = functools.partial(pltpu.with_memory_space_constraint, memory_space=pltpu.HBM)
    in_vmem = functools.partial(pltpu.with_memory_space_constraint, memory_space=pltpu.VMEM)
    offsets = in_hbm(offsets)
    send, meta = pl.pallas_call(
        gather_kernel,
        out_shape=(pltpu.VMEM(by_peer, BF16), pltpu.VMEM((RES, 1, 128), F32)),
        in_specs=[scalars, whole, anywhere, anywhere],
        out_specs=(anywhere, whole),
        scratch_shapes=[vmem((36, RES * 128), F32), dma((NPEER,)), dma],
        compiler_params=pltpu.CompilerParams(vmem_limit_bytes=SMALL_VMEM),
    )(
        offsets,
        in_hbm(coefs),
        in_hbm(jnp.asarray(to_local_table(tile))),
        in_hbm(dirty.reshape(footprint)),
    )
    joint, back = pl.pallas_call(
        kernel,
        out_shape=(pltpu.VMEM(image, BF16), pltpu.VMEM(by_peer, BF16)),
        in_specs=[anywhere, anywhere],
        out_specs=(anywhere, anywhere),
        scratch_shapes=[
            vmem(tiles, BF16),
            vmem(tiles, BF16),
            vmem(tiles, BF16),
            vmem(tiles, BF16),
            vmem((NPEER, 1, 128), F32),
            vmem((NPEER, 1, 128), F32),
            vmem((2, NPEER * 8, 128), F32),
            vmem((2, NPEER * GR, 128), BF16),
            vmem((2, NPEER * 8, tile), F32),
            vmem((256, NPEER * GR), BF16),
            vmem((3, 256, 256), BF16),
            vmem((NPEER * GR, 256), BF16),
            vmem((NPEER * GR, tile), BF16),
            vmem((NPEER * GR, tile), BF16),
            vmem((strips, 4, NT * GR, tile), F32),
            vmem((strips, 4, SHARED, tile), F32),
            vmem((strips, 2, 2 * FT * GR, tile), BF16),
            vmem((strips, 2, 2 * FT * GR, tile), BF16),
            vmem((strips, 3, NT * GR, tile), BF16),
            vmem((strips, 2, FT, GR, tile), BF16),
            dma((strips,)),
            dma((strips,)),
            dma((strips, 3)),
            dma((2,)),
            dma((2,)),
            dma((4,)),
            dma((strips,)),
            dma((strips,)),
            dma((strips, 2)),
            dma((strips, 2)),
            dma((strips, 2)),
            dma((strips, 2)),
            dma((strips,)),
            dma((strips,)),
            dma((strips,)),
            dma((strips,)),
            dma((strips,)),
            dma((strips,)),
            dma((strips,)),
            dma((strips, 3)),
        ],
        compiler_params=pltpu.CompilerParams(
            collective_id=0, has_side_effects=True, vmem_limit_bytes=MAIN_VMEM
        ),
    )(in_vmem(send), in_vmem(meta))
    joint, residual = pl.pallas_call(
        place_kernel,
        out_shape=(pltpu.HBM(image, BF16), pltpu.HBM(footprint, BF16)),
        in_specs=[scalars, anywhere, anywhere],
        out_specs=(anywhere, anywhere),
        scratch_shapes=[dma((NPEER + 1,))],
        compiler_params=pltpu.CompilerParams(vmem_limit_bytes=SMALL_VMEM),
    )(offsets, in_vmem(joint), in_vmem(back))
    return joint, residual.reshape(1, foot, foot)


def solution(mesh):
    in_specs = (P(("row", "col"), None, None), P(("row", "col"), None), P(("row", "col"), None))
    out_specs = (P("row", "col", None, None), P(("row", "col"), None, None))
    return jax.shard_map(
        local, mesh=mesh, in_specs=in_specs, out_specs=out_specs, check_vma=False
    )
```
